128 devices in a mesh: dp: 32 (over y, z, core), tensor: 4 (over x).
Axes of the slice: x: 4, y: 4, z: 4, core: 2. Of those that a mesh axis runs over, the one named last changes fastest.
Arguments:
- block_input: float32 [32768, 768], P('dp'), may hold values from -6 to 6
- lengths: int32 [32], P('dp'), may hold values from 1 to 1024, 22528 in all
- cotangent: float32 [32768, 768], P('dp'), may hold values from -6 to 6
- w_query: bfloat16 [2, 768, 768], P(None, None, 'tensor'), may hold values from -0.21875 to 0.21875
- w_key: bfloat16 [2, 768, 768], P(None, None, 'tensor'), may hold values from -0.21875 to 0.21875
- w_value: bfloat16 [2, 768, 768], P(None, None, 'tensor'), may hold values from -0.21875 to 0.21875
- w_output: bfloat16 [2, 768, 768], P(None, 'tensor'), may hold values from -3 to 3
- w_gate: bfloat16 [2, 768, 2048], P(None, None, 'tensor'), may hold values from -0.21875 to 0.21875
- w_up: bfloat16 [2, 768, 2048], P(None, None, 'tensor'), may hold values from -0.21875 to 0.21875
- w_down: bfloat16 [2, 2048, 768], P(None, 'tensor'), may hold values from -0.125 to 0.125
- gains: float32 [4, 768], replicated, may hold values from 0.5 to 1.5
Outputs:
- block_output: float32 [32768, 768], P('dp')
- input_grad: float32 [32768, 768], P('dp')
- query_grad: float32 [2, 768, 768], P(None, 'dp', 'tensor')
- key_grad: float32 [2, 768, 768], P(None, 'dp', 'tensor')
- value_grad: float32 [2, 768, 768], P(None, 'dp', 'tensor')
- output_grad: float32 [2, 768, 768], P(None, 'tensor', 'dp')
- gate_grad: float32 [2, 768, 2048], P(None, 'dp', 'tensor')
- up_grad: float32 [2, 768, 2048], P(None, 'dp', 'tensor')
- down_grad: float32 [2, 2048, 768], P(None, 'tensor', 'dp')
- gain_grads: float32 [3, 768], P(None, 'dp')
- ffn_gain_grad: float32 [768], P('dp')
The draws below stay inside these ranges and needn't reach their ends.
Inputs may be any that keep to these rules, and one draw needn't show every extreme that they name: The 32 lengths sum to 22528, and the longest is exactly 1024.
All inputs are finite; a program needn't handle non-finite values. No bound on the sum of `lengths` on one device may be relied on, other than what follows from the above.
Results may differ from the reference program's by a relative error of at most 0.025.
The reference program's roundings to bfloat16 on the way count: a program that leaves them out, or rounds other values in their place, can miss the bound.
Values sent between devices are 32-bit elements; how exact they have to be, the bound alone decides.
A program may use at most 256 MiB of HBM per device.

```python
import math
import jax
import jax.numpy as jnp
import numpy as np
from jax import lax

D = 768
HEADS = 12
HEAD_DIM = 64
FF = 2048
SEQ = 1024
LAYERS = 2
ROWS = 32
TOKENS = 32768
N_DP = 32


def spiked(drawn, rng, source, target, parts, factor):
    def block_of(axis_at):
        return (jnp.arange(drawn.shape[axis_at]) // (drawn.shape[axis_at] // parts)).reshape((-1,) + (1,) * (drawn.ndim - 1 - axis_at))

    first = jax.random.permutation(rng, parts)[block_of(target)]
    other_side = (block_of(target) + parts // 2) % parts
    return jnp.where((block_of(source) == first) | (block_of(source) == other_side), factor * drawn, drawn)


def block_levels(key, extent, split, low, largest):
    def one(axis_at, parts):
        draws = jax.random.uniform(jax.random.fold_in(jax.random.fold_in(key, 6), axis_at), (parts,), jnp.float32, low / len(split), largest / len(split))
        return jnp.repeat(jnp.exp(draws), extent[axis_at] // parts).reshape((-1,) + (1,) * (len(extent) - axis_at - 1))

    level = one(*split[0])
    for cut in split[1:]:
        level = level * one(*cut)
    return level


def split_up(count, total, reach, lean):
    loads = [(1 << 20) // math.isqrt(grade ** lean) + 1 for grade in range(2, count + 1)]
    spare, holding = total - reach - (count - 1), [1] * (count - 1)
    while spare > 0:
        free = [i for i in range(count - 1) if holding[i] < reach]
        pool, left = sum([loads[i] for i in free]), spare
        for i in free:
            extra = min(reach - holding[i], max(1, left * loads[i] // pool), spare)
            holding[i] = holding[i] + extra
            spare = spare - extra
    return np.array([reach] + holding)


def uneven_parts(own_key, count, total, most, slope):
    if count == 2:
        one = jax.random.randint(own_key, (), max(1, total - most), min(most, total - 1) + 1)
        return jnp.stack([one, total - one])
    sizes = jnp.asarray(split_up(count, total, most, slope), jnp.int32)
    pairs = (count - 1) // 2
    donor, sink = sizes[1:1 + 2 * pairs:2], sizes[2:2 + 2 * pairs:2]
    margin = jnp.minimum(donor - 1, most - sink)
    moved = jax.random.randint(jax.random.fold_in(own_key, 1), (pairs,), 0, 1 << 20) % (margin + 1)
    sizes = sizes.at[1:1 + 2 * pairs:2].set(donor - moved).at[2:2 + 2 * pairs:2].set(sink + moved)
    return sizes[jax.random.permutation(jax.random.fold_in(own_key, 2), count)]


def centred(key, extent, spread, reach, split=(), kind=jnp.bfloat16):
    drawn = spread * jax.random.normal(key, extent, jnp.float32)
    if split:
        drawn = drawn * block_levels(key, extent, split, -0.22, 0.18)
    return jnp.clip(drawn, -reach, reach).astype(kind)


def bell_draw_with(stream_key, extent, scale, bound, cuts, heavy, kind=jnp.bfloat16):
    values = scale * jax.random.normal(stream_key, extent, jnp.float32)
    if cuts:
        values = values * block_levels(stream_key, extent, cuts, -0.22, 0.18)
    return jnp.clip(spiked(values, jax.random.fold_in(stream_key, 3), *heavy), -bound, bound).astype(kind)


def setup_inputs(seed: int = 0) -> dict:
    arg_keys = jax.random.split(jax.random.key(seed), 12)
    return {
        "block_input": bell_draw_with(arg_keys[0], (TOKENS, D), 1.0, 6.0, ((0, 32),), (0, 1, 32, 2.75), jnp.float32),
        "lengths": uneven_parts(arg_keys[1], ROWS, 11 * N_DP * SEQ // 16, SEQ, 2).astype(jnp.int32),
        "cotangent": bell_draw_with(arg_keys[2], (TOKENS, D), 1.0, 6.0, ((0, 32),), (0, 1, 32, 2.75), jnp.float32),
        "w_query": centred(arg_keys[3], (LAYERS, D, D), D ** -0.5, 0.21875, ((2, 4),)),
        "w_key": centred(arg_keys[4], (LAYERS, D, D), D ** -0.5, 0.21875, ((2, 4),)),
        "w_value": centred(arg_keys[5], (LAYERS, D, D), D ** -0.5, 0.21875, ((2, 4),)),
        "w_output": centred(arg_keys[6], (LAYERS, D, D), (max(D * 4 // SEQ, 4)) ** -0.5, 3.0, ((1, 4),)),
        "w_gate": centred(arg_keys[7], (LAYERS, D, FF), D ** -0.5, 0.21875, ((2, 4),)),
        "w_up": centred(arg_keys[8], (LAYERS, D, FF), D ** -0.5, 0.21875, ((2, 4),)),
        "w_down": centred(arg_keys[9], (LAYERS, FF, D), FF ** -0.5, 0.125, ((1, 4),)),
        "gains": jnp.clip(1.0 + 0.1 * jax.random.normal(arg_keys[10], (2 * LAYERS, D), jnp.float32), 0.5, 1.5),
    }


@jax.custom_vjp
def low(v):
    return lax.optimization_barrier(v.astype(jnp.bfloat16)).astype(jnp.float32)

@jax.custom_vjp
def low_back(v):
    return v

def low_keep(v):
    return (low(v), None)

def low_pass(kept, grad):
    return (grad,)

def back_keep(v):
    return (v, None)

def back_low(kept, grad):
    return (low(grad),)
low.defvjp(low_keep, low_pass)
low_back.defvjp(back_keep, back_low)
negative = -1e+30
highest = lax.Precision.HIGHEST

def rope_tables():
    half = HEAD_DIM // 2
    freq = 10000.0 ** (-jnp.arange(half, dtype=jnp.float32) * 2.0 / HEAD_DIM)
    angle = jnp.arange(SEQ, dtype=jnp.float32)[:, None] * freq[None, :]
    cosine = jnp.concatenate([jnp.cos(angle), jnp.cos(angle)], axis=1)
    sine = jnp.concatenate([jnp.sin(angle), jnp.sin(angle)], axis=1)
    return (cosine[:, None, :], sine[:, None, :])

def rotate(values, cosine, sine):
    half = HEAD_DIM // 2
    turned = jnp.concatenate([-values[..., half:], values[..., :half]], axis=-1)
    return values * cosine + turned * sine

def rmsnorm(resid, gain):
    return resid * lax.rsqrt(lax.optimization_barrier(jnp.mean(resid * resid, axis=-1, keepdims=True)) + 1e-05) * gain

def sequence_attend(pieces):
    queries, keys, values, length = pieces
    raw = jnp.einsum('shd,thd->hst', queries, keys, precision=highest) * HEAD_DIM ** (-0.5)
    scores = low_back(raw)
    rows = jnp.arange(SEQ, dtype=jnp.int32)[:, None]
    cols = jnp.arange(SEQ, dtype=jnp.int32)[None, :]
    allowed = (cols <= rows) & (cols < length)
    probs = low(jax.nn.softmax(jnp.where(allowed[None], scores, negative), axis=-1))
    mixed = jnp.einsum('hst,thd->shd', probs, values, precision=highest)
    return low(low_back(mixed))

def attention(inputs, w_q, w_k, w_v, w_o, cosine, sine, lengths):

    def project(weight):
        return low_back(jnp.dot(inputs, weight, precision=highest)).reshape(N_DP, SEQ, HEADS, HEAD_DIM)
    queries = low(rotate(project(w_q), cosine, sine))
    keys = low(rotate(project(w_k), cosine, sine))
    values = low(project(w_v))
    mixed = lax.map(jax.checkpoint(sequence_attend), (queries, keys, values, lengths))
    mixed = mixed.reshape(N_DP * SEQ, D)
    return low_back(jnp.dot(mixed, w_o, precision=highest))

def feed_forward(inputs, w_g, w_u, w_d):
    gate = low_back(jnp.dot(inputs, w_g, precision=highest))
    up = low_back(jnp.dot(inputs, w_u, precision=highest))
    hidden = low(jax.nn.silu(gate) * up)
    return low_back(jnp.dot(hidden, w_d, precision=highest))

def reference(block_input, lengths, cotangent, w_query, w_key, w_value, w_output, w_gate, w_up, w_down, gains):
    cosine, sine = rope_tables()
    positions = jnp.arange(SEQ, dtype=jnp.int32)[None, :]
    live = (positions < lengths[:, None]).astype(jnp.float32).reshape(N_DP * SEQ, 1)

    def forward(x, wq, wk, wv, wo, wg, wu, wd, gn):
        attn0 = attention(low(x), wq[0], wk[0], wv[0], wo[0], cosine, sine, lengths)
        hidden_state = rmsnorm(x + attn0, gn[0])
        ffn0 = feed_forward(low(hidden_state), wg[0], wu[0], wd[0])
        layer_out = rmsnorm(hidden_state + ffn0, gn[1])
        attn1 = attention(low(rmsnorm(layer_out, gn[2])), wq[1], wk[1], wv[1], wo[1], cosine, sine, lengths)
        middle = layer_out + attn1
        ffn1 = feed_forward(low(rmsnorm(middle, gn[3])), wg[1], wu[1], wd[1])
        return (middle + ffn1) * live
    weights = [w.astype(jnp.float32) for w in (w_query, w_key, w_value, w_output, w_gate, w_up, w_down)]
    result, pullback = jax.vjp(forward, block_input, *weights, gains)
    grads = pullback(cotangent)
    return (result, grads[0], grads[1], grads[2], grads[3], grads[4], grads[5], grads[6], grads[7], grads[8][:3], grads[8][3])
```

```python
import math

import jax
import jax.numpy as jnp
from jax import lax
from jax.experimental import pallas as pl
from jax.experimental.pallas import tpu as pltpu
from jax.sharding import PartitionSpec as P

bf, f32 = jnp.bfloat16, jnp.float32
MESH = pl.DeviceIdType.MESH

CHUNKS, ROWS, D, S, T = 12, 384, 768, 1024, 256
NB = S // T
HALF, QUART, PIECE = ROWS // 2, ROWS // 4, ROWS // 16
UNIT = 128 * 4
SCALE2 = 0.125 * math.log2(math.e)
EPS = 1e-5
NEG = -1e30


def nt(a, b):
    return lax.dot_general(a, b, (((1,), (1,)), ((), ())), preferred_element_type=f32)


def nn(a, b):
    return lax.dot_general(a, b, (((1,), (0,)), ((), ())), preferred_element_type=f32)


def lane(shape):
    return lax.broadcasted_iota(jnp.int32, shape, len(shape) - 1)


def line(shape):
    return lax.broadcasted_iota(jnp.int32, shape, len(shape) - 2)


def loop(count, body):
    lax.fori_loop(0, count, lambda i, c: (body(i), c)[1], 0)


def block(t, size=T):
    return pl.ds(pl.multiple_of(t * size, size), size)


def place():
    d = lax.axis_index("dp")
    return lax.axis_index("tensor"), d // 8, (d // 2) % 4, d % 2


def device(x, y, z, c):
    return (((y % 4) * 4 + (z % 4)) * 2 + c, x % 4)


def remote(src, dst, send, recv, to):
    return pltpu.make_async_remote_copy(
        src_ref=src, dst_ref=dst, send_sem=send, recv_sem=recv, device_id=to, device_id_type=MESH
    )


def greet():
    x, y, z, c = place()
    bar = pltpu.get_barrier_semaphore()
    for to in (
        device(x + 1, y, z, c),
        device(x + 2, y, z, c),
        device(x + 3, y, z, c),
        device(x, y + 1, z, c),
        device(x, y + 3, z, c),
        device(x, y, z + 1, c),
        device(x, y, z + 3, c),
        device(x, y, z, 1 - c),
    ):
        pl.semaphore_signal(bar, inc=1, device_id=to, device_id_type=MESH)
    pl.semaphore_wait(bar, 8)


class Gather:
    SEMS = [(CHUNKS, 2, 3)] * 2 + [(CHUNKS, 2, 2)] * 4 + [(CHUNKS,)] * 2
    BOTH = [(p, d) for p in (0, 1) for d in (0, 1)]

    def __init__(self, own, full, sems):
        self.own, self.full = own, full
        self.xs, self.xr, self.as_, self.ar, self.bs, self.br, self.cs, self.cr = sems
        self.at = place()

    def rows(self, p, pos):
        c = self.at[3]
        return pl.ds(pl.multiple_of(c * HALF + p * QUART + ((pos + 4) % 4) * PIECE, 8), PIECE)

    def near(self, p, step):
        x, y, z, c = self.at
        return device(x, y + 4 + step, z, c) if p == 0 else device(x, y, z + 4 + step, c)

    def x_copy(self, ch, p, rel):
        x, y, z, c = self.at
        here = self.rows(p, self.at[1 + p])
        return remote(
            self.own.at[ch, here],
            self.full.at[ch, rel - 1, here],
            self.xs.at[ch, p, rel - 1],
            self.xr.at[ch, p, rel - 1],
            device(x + 4 - rel, y, z, c),
        )

    def a_copy(self, ch, p, d, arriving=False):
        step = 1 - 2 * d
        pos = self.at[1 + p] - step if arriving else self.at[1 + p]
        ref = self.full.at[ch, :, self.rows(p, pos)]
        return remote(ref, ref, self.as_.at[ch, p, d], self.ar.at[ch, p, d], self.near(p, step))

    def b_copy(self, ch, p, d, arriving=False):
        step = 1 - 2 * d
        pos = self.at[1 + p] - 2 if arriving else self.at[1 + p] - step
        ref = self.full.at[ch, :, self.rows(p, pos), pl.ds(d * (D // 2), D // 2)]
        return remote(ref, ref, self.bs.at[ch, p, d], self.br.at[ch, p, d], self.near(p, step))

    def c_copy(self, ch, arriving=False):
        x, y, z, c = self.at
        half = 1 - c if arriving else c
        ref = self.full.at[ch, :, pl.ds(pl.multiple_of(half * HALF, 8), HALF)]
        return remote(ref, ref, self.cs.at[ch], self.cr.at[ch], device(x, y, z, 1 - c))

    def begin(self):
        def send(ch):
            for p in (0, 1):
                for rel in (1, 3, 2):
                    self.x_copy(ch, p, rel).start()

        loop(CHUNKS, send)

    def advance(self, k):
        @pl.when(k < CHUNKS)
        def _():
            for p in (0, 1):
                for rel in (1, 2, 3):
                    self.x_copy(k, p, rel).wait_recv()
            for p, d in self.BOTH:
                self.a_copy(k, p, d).start()

        @pl.when((k >= 1) & (k < CHUNKS + 1))
        def _():
            for p, d in self.BOTH:
                self.a_copy(k - 1, p, d, True).wait_recv()
            for p, d in self.BOTH:
                self.b_copy(k - 1, p, d).start()

        @pl.when((k >= 2) & (k < CHUNKS + 2))
        def _():
            for p, d in self.BOTH:
                self.b_copy(k - 2, p, d, True).wait_recv()
            self.c_copy(k - 2).start()

    def arrive(self, ch):
        self.c_copy(ch, True).wait_recv()

    def end(self):
        def sent(ch):
            for p in (0, 1):
                for rel in (1, 2, 3):
                    self.x_copy(ch, p, rel).wait_send()
            for p, d in self.BOTH:
                self.a_copy(ch, p, d).wait_send()
                self.b_copy(ch, p, d).wait_send()
            self.c_copy(ch).wait_send()

        loop(CHUNKS, sent)


class Nowhere:
    begin = end = lambda self: None
    advance = arrive = lambda self, k: None


PAIR_AT = (0, 256, 384, 512)
THIRD_AT = (128, 192, 640, 704)


def repack_heads(st, wb):
    for a in range(2):
        for r in range(4):
            to, third = a * 768 + PAIR_AT[r], a * 768 + THIRD_AT[r]
            wb[to : to + 128] = st[r, a * 192 : a * 192 + 128].astype(bf)
            wb[third : third + 64] = st[r, a * 192 + 128 : a * 192 + 192].astype(bf)


def repack_hidden(st, wb):
    for a in range(3):
        for r in range(4):
            to = a * 512 + r * 128
            wb[to : to + 128] = st[r, a * 128 : a * 128 + 128].astype(bf)


def transpose_to(dst, src):
    for t in range(NB):
        dst[:, t * T : (t + 1) * T] = src[t * T : (t + 1) * T, :].T


def rms(r):
    return lax.rsqrt(jnp.mean(r * r, axis=-1, keepdims=True) + EPS)


def rope(v, cs, sl, sr):
    return v * cs + pltpu.roll(v, 96, 1) * sl + pltpu.roll(v, 32, 1) * sr


def rope_sides(sn):
    first = (lane(sn.shape) % 64) < 32
    return jnp.where(first, -sn, 0.0), jnp.where(first, 0.0, sn)


def head_lanes(h, shape):
    at = lane(shape)
    mine = at < 64 if h == 0 else at >= 64
    base = 64 if h == 0 else 0
    return mine, at - base


def project(u, wqk, wv, cs, sn, length, qa, ka, va, v, k):
    def step(t):
        at = block(t)
        ut = u[at]
        c = cs[at]
        sl, sr = rope_sides(sn[at])
        shape = (T, 128)
        bias = jnp.where(line(shape) + t * T < length, 0.0, NEG)
        val = nt(ut, wqk[0:768])
        for p in range(6):
            q_p = rope(val[:, p * 128 : p * 128 + 128], c, sl, sr)
            for h in range(2):
                mine, side = head_lanes(h, shape)
                qa[2 * p + h, at] = jnp.where(mine, q_p, jnp.where(side == 0, 1.0, 0.0)).astype(bf)
        val = nt(ut, wqk[768:1536])
        for p in range(6):
            k_p = rope(val[:, p * 128 : p * 128 + 128], c, sl, sr)
            k[p, at] = k_p.astype(bf)
            for h in range(2):
                mine, side = head_lanes(h, shape)
                other = jnp.where(side == 0, bias, jnp.where(side < 4, -1.0, 0.0))
                ka[2 * p + h, at] = jnp.where(mine, k_p, other).astype(bf)
        val = nt(ut, wv[0:768])
        for p in range(6):
            v_p = val[:, p * 128 : p * 128 + 128]
            v[p, at] = v_p.astype(bf)
            for h in range(2):
                mine, side = head_lanes(h, shape)
                va[2 * p + h, at] = jnp.where(mine, v_p, jnp.where((side >= 1) & (side < 4), -1.0, 0.0)).astype(bf)

    loop(NB, step)


def attend(qa, ka, vt, o, ob, lse, tick):
    def pair(p):
        at_l = pl.ds(pl.multiple_of(p * 128, 128), 128)
        for i in range(NB):
            n = (i + 1) * T
            rows = pl.ds(i * T, T)
            diag = line((T, T)) <= lane((T, T))
            outs, outl = [], []
            for h in range(2):
                s = nt(ka[2 * p + h, 0:n], qa[2 * p + h, rows])
                tail = jnp.where(diag, s[n - T :], NEG)
                s = tail if i == 0 else jnp.concatenate([s[: n - T], tail], axis=0)
                m = jnp.max(s, axis=0, keepdims=True) * SCALE2
                e = jnp.exp2(s * SCALE2 - m)
                tot = jnp.sum(e, axis=0, keepdims=True)
                pr = e * (1.0 / tot)
                pb = pr.astype(bf)
                main = nn(vt[p, h * 64 : h * 64 + 64, 0:n], pb)
                rest = (pr - pb.astype(f32)).astype(bf)
                outs.append(main)
                outl.append(main + nn(vt[p, h * 64 : h * 64 + 64, 0:n], rest))
                lse[pl.ds(p * 2 + h, 1), rows] = m + jnp.log2(tot)
            ob[rows, at_l] = jnp.concatenate(outs, axis=0).T.astype(bf)
            o[rows, at_l] = jnp.concatenate(outl, axis=0).T
        tick(p)

    loop(6, pair)


def three(v):
    hi = v.astype(bf).astype(f32)
    mid = (v - hi).astype(bf).astype(f32)
    low = (v - hi - mid).astype(bf).astype(f32)
    return (hi + pltpu.roll(mid, 16, 1) + pltpu.roll(low, 32, 1)).astype(bf)


def spread_table():
    shape = (128, 12 * 128)
    r, c = line(shape), lane(shape)
    h, at = c // 128, c % 128
    j = at - jnp.where(h % 2 == 0, 65, 1)
    return jnp.where((j >= 0) & (j < 3) & (r == 16 * j + h), 1.0, 0.0).astype(bf)


FWD_OUT = [
    ((CHUNKS, 1536, D), bf),
    ((2, 2, D, S), bf),
    ((2, 12, S, 128), bf),
    ((2, 12, S, 128), bf),
    ((2, 12, S, 128), bf),
    ((2, 6, 128, S), bf),
    ((2, S, D), f32),
    ((2, S, 256), bf),
    ((2, 4, S, 512), f32),
    ((2, 4, S, 512), f32),
    ((2, 4, S, 128), bf),
    ((4, S, D), f32),
    ((S, D), f32),
]
FWD_VMEM = [
    ((S, D), f32),
    ((2, 4, ROWS, D), f32),
    ((2, 1536, D), bf),
    ((12, S, 128), bf),
    ((12, S, 128), bf),
    ((12, S, 128), bf),
    ((6, S, 128), bf),
    ((6, S, 128), bf),
    ((6, 128, S), bf),
    ((6, 128, S), bf),
    ((S, D), f32),
    ((S, D), bf),
    ((128, S), f32),
    ((S, D), bf),
    ((2, D, S), bf),
    ((S, D), f32),
    ((S, D), f32),
    ((2, 2, 512, 512), f32),
    ((4, S, 128), bf),
]


def fwd_kernel(comm, length_ref, own, x_hbm, cs, sn, gains, spread, *rest):
    if comm:
        full, rest = rest[0], rest[1:]
    else:
        full, rest = spread, rest
        spread, rest = rest[0], rest[1:]
    outs, rest = rest[: len(FWD_OUT)], rest[len(FWD_OUT) :]
    w_o, ut_o, qa_o, ka_o, va_o, kt_o, o_o, ob_o, a_o, b_o, hb_o, res_o, out_o = outs
    (x, st, wb, qa, ka, va, k, v, kt, vt, o, ob, lse, u, ut, acc, res, ab, hb), rest = (
        rest[: len(FWD_VMEM)],
        rest[len(FWD_VMEM) :],
    )
    load_sem, w_sem, save_sem, ab_sem = rest[:4]
    net = Gather(own, full, rest[4:]) if comm else Nowhere()
    length = length_ref[0]

    x_in = pltpu.make_async_copy(x_hbm, x, save_sem.at[0])
    x_in.start()
    if comm:
        greet()
    net.begin()
    x_in.wait()

    def loads(ch, slot):
        return (
            pltpu.make_async_copy(own.at[ch], st.at[slot, 0], load_sem.at[slot, 0]),
            pltpu.make_async_copy(full.at[ch], st.at[slot, pl.ds(1, 3)], load_sem.at[slot, 1]),
        )

    def start_load(ch, slot):
        net.arrive(ch)
        for copy in loads(ch, slot):
            copy.start()

    def put_weights(ch, slot):
        return pltpu.make_async_copy(wb.at[slot], w_o.at[ch], w_sem.at[slot])

    def unpack(ch, slot, repack, first=False):
        for copy in loads(ch, slot):
            copy.wait()
        if not first:
            put_weights(ch, slot).wait()
        repack(st.at[slot], wb.at[slot])
        put_weights(ch, slot).start()

    flying = {}

    def save(name, src, dst, i):
        flying[name] = pltpu.make_async_copy(src, dst, save_sem.at[i])
        flying[name].start()

    def settle(*names):
        for name in names:
            if name in flying:
                flying.pop(name).wait()

    loop(4, net.advance)
    start_load(0, 0)
    start_load(1, 1)
    lse[...] = jnp.zeros((128, S), f32)
    for layer in range(2):
        base = layer * 6
        settle("uta")
        net.advance(base + 4 if layer == 0 else 11)

        def enter(t):
            at = block(t)
            val = x[at]
            if layer:
                val = val * rms(val) * gains[2:3]
            u[at] = val.astype(bf)

        loop(NB, enter)
        transpose_to(ut.at[0], u)
        save("uta", ut.at[0], ut_o.at[layer, 0], 0)
        unpack(base, 0, repack_heads, layer == 0)
        unpack(base + 1, 1, repack_heads, layer == 0)
        start_load(base + 2, 0)
        settle("qa", "ka", "va", "kt", "o", "ob")
        project(u, wb.at[0], wb.at[1], cs, sn, length, qa, ka, va, v, k)
        for p in range(6):
            transpose_to(kt.at[p], k.at[p])
            transpose_to(vt.at[p], v.at[p])
        save("ka", ka, ka_o.at[layer], 1)
        save("va", va, va_o.at[layer], 2)
        save("kt", kt, kt_o.at[layer], 3)
        net.advance(5 if layer == 0 else 12)

        def tick(p):
            @pl.when(lax.rem(p, 2) == 1)
            def _():
                net.advance((6 if layer == 0 else 13) + p // 2)

        attend(qa, ka, vt, o, ob, lse, tick)
        save("o", o, o_o.at[layer], 4)
        save("ob", ob.at[:, pl.ds(0, 256)], ob_o.at[layer], 5)

        def add_lse(t):
            at = block(t)
            val = nn(three(lse[:, at].T), spread[...])
            for h in range(12):
                qa[h, at] = (qa[h, at].astype(f32) + val[:, h * 128 : h * 128 + 128]).astype(bf)

        loop(NB, add_lse)
        save("qa", qa, qa_o.at[layer], 6)
        settle("res")

        def after(t):
            at = block(t)
            r = x[at] + nn(ob[at], wb[1, 768:1536])
            res[at] = r
            n = r * rms(r)
            if layer == 0:
                h = n * gains[0:1]
                acc[at] = h
                u[at] = h.astype(bf)
            else:
                acc[at] = r
                u[at] = (n * gains[3:4]).astype(bf)

        loop(NB, after)
        save("res", res, res_o.at[2 * layer if layer == 0 else 3], 7)
        settle("utf")
        transpose_to(ut.at[1], u)
        save("utf", ut.at[1], ut_o.at[layer, 1], 8)
        settle("hb")

        def chunk(f):
            ch = base + 2 + f
            slot = lax.rem(f, 2)

            @pl.when(ch + 1 < CHUNKS)
            def _():
                start_load(ch + 1, 1 - slot)

            if layer == 0:

                @pl.when(lax.rem(f, 2) == 0)
                def _():
                    net.advance(9 + f // 2)

            unpack(ch, slot, repack_hidden)
            w = wb.at[slot]

            def step(t):
                at = block(t, 512)

                def put(j):
                    return pltpu.make_async_copy(ab.at[t, j], (a_o, b_o)[j].at[layer, f, at], ab_sem.at[t, j])

                @pl.when(f >= 1)
                def _():
                    put(0).wait()
                    put(1).wait()

                ub = u[at]
                gate = nt(ub, w[0:512])
                up = nt(ub, w[512:1024])
                sig = 1.0 / (1.0 + jnp.exp(-gate))
                a = gate * sig
                hid = (a * up).astype(bf)
                ab[t, 0] = a
                ab[t, 1] = up * (sig + a * (1.0 - sig))
                hb[f, at] = hid[:, 0:128]
                acc[at] = acc[at] + nn(hid, w[1024:1536])
                put(0).start()
                put(1).start()

            loop(2, step)

        loop(4, chunk)
        for t in range(2):
            for j in range(2):
                pltpu.make_async_copy(ab.at[t, j], a_o.at[layer, 0, block(0, 512)], ab_sem.at[t, j]).wait()
        save("hb", hb, hb_o.at[layer], 9)
        if layer == 0:
            start_load(7, 1)
            settle("res")

            def leave(t):
                at = block(t)
                r = acc[at]
                res[at] = r
                x[at] = r * rms(r) * gains[1:2]

            loop(NB, leave)
            save("res", res, res_o.at[1], 7)
            save("y", x, res_o.at[2], 10)
        else:
            settle("y")

            def last(t):
                at = block(t)
                x[at] = jnp.where(line((T, 1)) + t * T < length, acc[at], 0.0)

            loop(NB, last)
            save("out", x, out_o, 11)
    settle(*list(flying))
    for slot in range(2):
        put_weights(0, slot).wait()
    net.end()


def whole(memory):
    return pl.BlockSpec(memory_space=memory)


def forward(length, own, x, cs, sn, gains, spread, full=None):
    comm = full is None
    hbm, vmem = whole(pl.ANY), whole(pltpu.VMEM)
    outs = [jax.ShapeDtypeStruct(s, d) for s, d in FWD_OUT]
    if comm:
        outs = [jax.ShapeDtypeStruct((CHUNKS, 3, ROWS, D), f32)] + outs
    dma = pltpu.SemaphoreType.DMA
    result = pl.pallas_call(
        lambda *refs: fwd_kernel(comm, *refs),
        out_shape=outs,
        in_specs=[whole(pltpu.SMEM), hbm, hbm, vmem, vmem, vmem] + ([] if comm else [hbm]) + [vmem],
        out_specs=[hbm] * len(outs),
        scratch_shapes=[pltpu.VMEM(s, d) for s, d in FWD_VMEM]
        + [dma((2, 2)), dma((2,)), dma((12,)), dma((2, 2))]
        + ([dma(s) for s in Gather.SEMS] if comm else []),
        compiler_params=pltpu.CompilerParams(
            vmem_limit_bytes=62 * 2**20,
            **(dict(collective_id=0, has_side_effects=True) if comm else {}),
        ),
    )(length, own, x, cs, sn, gains, *([] if comm else [full]), spread)
    return result[1:] if comm else result


def pack_own(wq, wk, wv, wo, wg, wu, wd):
    parts = []
    for layer in range(2):
        parts += [wq[layer].T, wk[layer].T, wv[layer].T, wo[layer]]
        gate, up, down = wg[layer].T, wu[layer].T, wd[layer]
        for f in range(4):
            part = slice(f * 128, f * 128 + 128)
            parts += [gate[part], up[part], down[part]]
    return jnp.concatenate(parts).astype(f32).reshape(CHUNKS, ROWS, D)


def rope_tables(count):
    freq = 10000.0 ** (-jnp.arange(32, dtype=f32) * 2.0 / 64)
    angle = jnp.arange(count, dtype=f32)[:, None] * freq[None, :]
    cosine, sine = jnp.cos(angle), jnp.sin(angle)
    return jnp.concatenate([cosine] * 4, axis=1), jnp.concatenate([sine] * 4, axis=1)

HEAD_DIM = 64


negative = -1e30
epsilon = 1e-05


def split_up(value, dim, peers):
    shape = value.shape
    blocks = value.reshape(*shape[:dim], peers, shape[dim] // peers, *shape[dim + 1 :])
    return jnp.moveaxis(blocks, dim, 0)


def sum_packed(arrays, axis, dims):
    peers = lax.axis_size(axis)
    blocks = [split_up(a, dim, peers) for a, dim in zip(arrays, dims)]
    lines = jnp.concatenate([b.reshape(peers, -1) for b in blocks], axis=1)
    extent = max(16, -(-lines.shape[1] // 1024) * 8)
    lines = jnp.pad(lines, ((0, 0), (0, extent * 128 - lines.shape[1]))).reshape(-1, 128)
    line, at, finished = (lax.psum_scatter(lines, axis, tiled=True).reshape(-1), 0, [])
    for b in blocks:
        part = b[0]
        finished.append(line[at : at + part.size].reshape(part.shape))
        at += part.size
    return tuple(finished)


def rope_tables0(count):
    half = HEAD_DIM // 2
    freq = 10000.0 ** (-jnp.arange(half, dtype=jnp.float32) * 2.0 / HEAD_DIM)
    angle = jnp.arange(count, dtype=jnp.float32)[:, None] * freq[None, :]
    cosine = jnp.concatenate([jnp.cos(angle), jnp.cos(angle)], axis=1)
    sine = jnp.concatenate([jnp.sin(angle), jnp.sin(angle)], axis=1)
    return (cosine[:, None, :], sine[:, None, :])


def rotate(values, cosine, sine):
    half = HEAD_DIM // 2
    turned = jnp.concatenate([-values[..., half:], values[..., :half]], axis=-1)
    return values * cosine + turned * sine


def unrotate(grads, cosine, sine):
    half = HEAD_DIM // 2
    scaled = grads * sine
    back = jnp.concatenate([scaled[..., half:], -scaled[..., :half]], axis=-1)
    return grads * cosine + back


def norm_forward(resid, gain):
    factor = lax.rsqrt(jnp.mean(resid * resid, axis=-1, keepdims=True) + epsilon)
    normed = resid * factor
    return (normed * gain, normed, factor)


def norm_backward(grad, normed, factor, gain):
    gain_grad = jnp.sum(grad * normed, axis=0)
    inner = grad * gain
    return (factor * (inner - normed * jnp.mean(inner * normed, axis=-1, keepdims=True)), gain_grad)


def branch_total(part):
    return lax.psum(part, "tensor")


def input_total(part):
    return lax.psum(part, "tensor")


def score_block(queries, keys, length):
    count = queries.shape[0]
    raw = jnp.einsum(
        "shd,thd->hst", queries, keys, preferred_element_type=jnp.float32
    ) * HEAD_DIM ** (-0.5)
    rows = jnp.arange(count, dtype=jnp.int32)[:, None]
    cols = jnp.arange(count, dtype=jnp.int32)[None, :]
    allowed = (cols <= rows) & (cols < length)
    return jnp.where(allowed[None], raw, negative)


def outer_sum(left, right):
    return jnp.einsum("sa,sb->ab", left, right, preferred_element_type=jnp.float32)


def back_product(grad, weight):
    return jnp.einsum("sb,ab->sa", grad, weight, preferred_element_type=jnp.float32)


def attend_forward(inputs, w_q, w_k, w_v, w_o, cosine, sine, length):
    count = inputs.shape[0]
    heads = w_q.shape[1] // HEAD_DIM

    def project(weight):
        return jnp.dot(inputs, weight, preferred_element_type=jnp.float32).reshape(
            count, heads, HEAD_DIM
        )

    queries = rotate(project(w_q), cosine, sine).astype(jnp.bfloat16)
    keys = rotate(project(w_k), cosine, sine).astype(jnp.bfloat16)
    values = project(w_v).astype(jnp.bfloat16)
    scores = score_block(queries, keys, length)
    peak = jnp.max(scores, axis=-1, keepdims=True)
    logsum = peak + jnp.log(jnp.sum(jnp.exp(scores - peak), axis=-1, keepdims=True))
    probs = jnp.exp(scores - logsum).astype(jnp.bfloat16)
    mixed = jnp.einsum("hst,thd->shd", probs, values, preferred_element_type=jnp.float32)
    mixed = mixed.reshape(count, heads * HEAD_DIM).astype(jnp.bfloat16)
    part = jnp.dot(mixed, w_o, preferred_element_type=jnp.float32)
    return (part, (inputs, queries, keys, values, mixed, logsum))


def attend_backward(grad, saved, w_q, w_k, w_v, w_o, cosine, sine, length):
    inputs, queries, keys, values, mixed, logsum = saved
    count = inputs.shape[0]
    heads = w_q.shape[1] // HEAD_DIM
    grad_low = grad.astype(jnp.bfloat16)
    grad_wo = outer_sum(mixed, grad_low)
    grad_mixed = back_product(grad_low, w_o).reshape(count, heads, HEAD_DIM).astype(jnp.bfloat16)
    probs = jnp.exp(score_block(queries, keys, length) - logsum)
    grad_probs = jnp.einsum("shd,thd->hst", grad_mixed, values, preferred_element_type=jnp.float32)
    inner = jnp.sum(probs * grad_probs, axis=-1, keepdims=True)
    grad_scores = (probs * (grad_probs - inner)).astype(jnp.bfloat16)
    grad_values = jnp.einsum(
        "hst,shd->thd", probs.astype(jnp.bfloat16), grad_mixed, preferred_element_type=jnp.float32
    )
    grad_values = grad_values.reshape(count, heads * HEAD_DIM).astype(jnp.bfloat16)
    grad_rq = jnp.einsum(
        "hst,thd->shd", grad_scores, keys, preferred_element_type=jnp.float32
    ) * HEAD_DIM ** (-0.5)
    grad_rk = jnp.einsum(
        "hst,shd->thd", grad_scores, queries, preferred_element_type=jnp.float32
    ) * HEAD_DIM ** (-0.5)
    grad_queries = (
        unrotate(grad_rq, cosine, sine).reshape(count, heads * HEAD_DIM).astype(jnp.bfloat16)
    )
    grad_keys = (
        unrotate(grad_rk, cosine, sine).reshape(count, heads * HEAD_DIM).astype(jnp.bfloat16)
    )
    grad_wq = outer_sum(inputs, grad_queries)
    grad_wk = outer_sum(inputs, grad_keys)
    grad_wv = outer_sum(inputs, grad_values)
    partial_value = (
        back_product(grad_queries, w_q)
        + back_product(grad_keys, w_k)
        + back_product(grad_values, w_v)
    )
    return (partial_value, (grad_wq, grad_wk, grad_wv, grad_wo))


def feed_forward(inputs, w_g, w_u, w_d):
    gate = jnp.dot(inputs, w_g, preferred_element_type=jnp.float32)
    up_val = jnp.dot(inputs, w_u, preferred_element_type=jnp.float32)
    hidden = (jax.nn.silu(gate) * up_val).astype(jnp.bfloat16)
    part = jnp.dot(hidden, w_d, preferred_element_type=jnp.float32)
    return (part, (inputs, gate, up_val, hidden))


def feed_backward(grad, saved, w_g, w_u, w_d):
    inputs, gate, up_val, hidden = saved
    grad_low = grad.astype(jnp.bfloat16)
    grad_wd = outer_sum(hidden, grad_low)
    grad_hidden = back_product(grad_low, w_d)
    sigma = jax.nn.sigmoid(gate)
    grad_gate = (grad_hidden * up_val * sigma * (1.0 + gate * (1.0 - sigma))).astype(jnp.bfloat16)
    grad_up = (grad_hidden * jax.nn.silu(gate)).astype(jnp.bfloat16)
    grad_wg = outer_sum(inputs, grad_gate)
    grad_wu = outer_sum(inputs, grad_up)
    partial_value = back_product(grad_gate, w_g) + back_product(grad_up, w_u)
    return (partial_value, (grad_wg, grad_wu, grad_wd))


def local(
    block_input, lengths, cotangent, w_query, w_key, w_value, w_output, w_gate, w_up, w_down, gains
):
    count = block_input.shape[0]
    length = lengths[0]
    cosine, sine = rope_tables0(count)
    live = (jnp.arange(count, dtype=jnp.int32) < length).astype(jnp.float32)[:, None]
    part, attn0 = attend_forward(
        block_input.astype(jnp.bfloat16),
        w_query[0],
        w_key[0],
        w_value[0],
        w_output[0],
        cosine,
        sine,
        length,
    )
    hidden_state, normed1, factor1 = norm_forward(block_input + branch_total(part), gains[0])
    part, ffn0 = feed_forward(hidden_state.astype(jnp.bfloat16), w_gate[0], w_up[0], w_down[0])
    layer_out, normed2, factor2 = norm_forward(hidden_state + branch_total(part), gains[1])
    pre_attn, normed3, factor3 = norm_forward(layer_out, gains[2])
    part, attn1 = attend_forward(
        pre_attn.astype(jnp.bfloat16),
        w_query[1],
        w_key[1],
        w_value[1],
        w_output[1],
        cosine,
        sine,
        length,
    )
    middle = layer_out + branch_total(part)
    pre_ffn, normed4, factor4 = norm_forward(middle, gains[3])
    part, ffn1 = feed_forward(pre_ffn.astype(jnp.bfloat16), w_gate[1], w_up[1], w_down[1])
    block_output = (middle + branch_total(part)) * live
    grad_final = cotangent * live
    part, ffn1_grads = feed_backward(grad_final, ffn1, w_gate[1], w_up[1], w_down[1])
    grad_mid_norm, gain3 = norm_backward(input_total(part), normed4, factor4, gains[3])
    grad_middle = grad_final + grad_mid_norm
    part, attn1_grads = attend_backward(
        grad_middle, attn1, w_query[1], w_key[1], w_value[1], w_output[1], cosine, sine, length
    )
    grad_out_norm, gain2 = norm_backward(input_total(part), normed3, factor3, gains[2])
    grad_layer_out = grad_middle + grad_out_norm
    grad_resid2, gain1 = norm_backward(grad_layer_out, normed2, factor2, gains[1])
    part, ffn0_grads = feed_backward(grad_resid2, ffn0, w_gate[0], w_up[0], w_down[0])
    grad_hidden = grad_resid2 + input_total(part)
    grad_resid1, gain0 = norm_backward(grad_hidden, normed1, factor1, gains[0])
    part, attn0_grads = attend_backward(
        grad_resid1, attn0, w_query[0], w_key[0], w_value[0], w_output[0], cosine, sine, length
    )
    input_grad = grad_resid1 + input_total(part)
    stacked = [jnp.stack([attn0_grads[index], attn1_grads[index]]) for index in range(4)]
    stacked = stacked + [jnp.stack([ffn0_grads[index], ffn1_grads[index]]) for index in range(3)]
    total = sum_packed(
        (
            stacked[0],
            stacked[1],
            stacked[2],
            stacked[3],
            stacked[4],
            stacked[5],
            stacked[6],
            jnp.stack([gain0, gain1, gain2, gain3]),
        ),
        "dp",
        (1, 1, 1, 2, 1, 1, 2, 1),
    )
    summed = [total[index] for index in range(7)]
    gain_grads = total[7][:3]
    ffn_gain_grad = total[7][3]
    cs, sn = rope_tables(count)
    kept = forward(lengths, pack_own(w_query, w_key, w_value, w_output, w_gate, w_up, w_down), block_input, cs, sn, gains, spread_table())
    block_output = kept[12]
    return (
        block_output,
        input_grad,
        summed[0],
        summed[1],
        summed[2],
        summed[3],
        summed[4],
        summed[5],
        summed[6],
        gain_grads,
        ffn_gain_grad,
    )


def solution(mesh):
    return jax.shard_map(
        local,
        mesh=mesh,
        in_specs=(
            P("dp", None),
            P("dp"),
            P("dp", None),
            P(None, None, "tensor"),
            P(None, None, "tensor"),
            P(None, None, "tensor"),
            P(None, "tensor", None),
            P(None, None, "tensor"),
            P(None, None, "tensor"),
            P(None, "tensor", None),
            P(),
        ),
        out_specs=(
            P("dp", None),
            P("dp", None),
            P(None, "dp", "tensor"),
            P(None, "dp", "tensor"),
            P(None, "dp", "tensor"),
            P(None, "tensor", "dp"),
            P(None, "dp", "tensor"),
            P(None, "dp", "tensor"),
            P(None, "tensor", "dp"),
            P(None, "dp"),
            P("dp"),
        ),
        check_vma=False,
    )
```

```python
import math

import jax
import jax.numpy as jnp
import ml_dtypes
import numpy as np
from jax import lax
from jax.experimental import pallas as pl
from jax.experimental.pallas import tpu as pltpu
from jax.sharding import PartitionSpec as P

bf, f32 = jnp.bfloat16, jnp.float32
MESH = pl.DeviceIdType.MESH

CHUNKS, ROWS, D, S, T = 12, 384, 768, 1024, 256
NB = S // T
HALF, QUART, PIECE = ROWS // 2, ROWS // 4, ROWS // 16
UNIT = 128 * 4
SCALE2 = 0.125 * math.log2(math.e)
EPS = 1e-5
NEG = -1e30


def nt(a, b):
    return lax.dot_general(a, b, (((1,), (1,)), ((), ())), preferred_element_type=f32)


def nn(a, b):
    return lax.dot_general(a, b, (((1,), (0,)), ((), ())), preferred_element_type=f32)


def lane(shape):
    return lax.broadcasted_iota(jnp.int32, shape, len(shape) - 1)


def line(shape):
    return lax.broadcasted_iota(jnp.int32, shape, len(shape) - 2)


def loop(count, body):
    lax.fori_loop(0, count, lambda i, c: (body(i), c)[1], 0)


def block(t, size=T):
    return pl.ds(pl.multiple_of(t * size, size), size)


def place():
    d = lax.axis_index("dp")
    return lax.axis_index("tensor"), d // 8, (d // 2) % 4, d % 2


def device(x, y, z, c):
    return (((y % 4) * 4 + (z % 4)) * 2 + c, x % 4)


def remote(src, dst, send, recv, to):
    return pltpu.make_async_remote_copy(
        src_ref=src, dst_ref=dst, send_sem=send, recv_sem=recv, device_id=to, device_id_type=MESH
    )


def greet():
    x, y, z, c = place()
    bar = pltpu.get_barrier_semaphore()
    for to in (
        device(x + 1, y, z, c),
        device(x + 2, y, z, c),
        device(x + 3, y, z, c),
        device(x, y + 1, z, c),
        device(x, y + 3, z, c),
        device(x, y, z + 1, c),
        device(x, y, z + 3, c),
        device(x, y, z, 1 - c),
    ):
        pl.semaphore_signal(bar, inc=1, device_id=to, device_id_type=MESH)
    pl.semaphore_wait(bar, 8)


class Gather:
    SEMS = [(CHUNKS, 2, 3)] * 2 + [(CHUNKS, 2, 2)] * 4 + [(CHUNKS,)] * 2
    BOTH = [(p, d) for p in (0, 1) for d in (0, 1)]

    def __init__(self, own, full, sems):
        self.own, self.full = own, full
        self.xs, self.xr, self.as_, self.ar, self.bs, self.br, self.cs, self.cr = sems
        self.at = place()

    def rows(self, p, pos):
        c = self.at[3]
        return pl.ds(pl.multiple_of(c * HALF + p * QUART + ((pos + 4) % 4) * PIECE, 8), PIECE)

    def near(self, p, step):
        x, y, z, c = self.at
        return device(x, y + 4 + step, z, c) if p == 0 else device(x, y, z + 4 + step, c)

    def x_copy(self, ch, p, rel):
        x, y, z, c = self.at
        here = self.rows(p, self.at[1 + p])
        return remote(
            self.own.at[ch, here],
            self.full.at[ch, rel - 1, here],
            self.xs.at[ch, p, rel - 1],
            self.xr.at[ch, p, rel - 1],
            device(x + 4 - rel, y, z, c),
        )

    def a_copy(self, ch, p, d, arriving=False):
        step = 1 - 2 * d
        pos = self.at[1 + p] - step if arriving else self.at[1 + p]
        ref = self.full.at[ch, :, self.rows(p, pos)]
        return remote(ref, ref, self.as_.at[ch, p, d], self.ar.at[ch, p, d], self.near(p, step))

    def b_copy(self, ch, p, d, arriving=False):
        step = 1 - 2 * d
        pos = self.at[1 + p] - 2 if arriving else self.at[1 + p] - step
        ref = self.full.at[ch, :, self.rows(p, pos), pl.ds(d * (D // 2), D // 2)]
        return remote(ref, ref, self.bs.at[ch, p, d], self.br.at[ch, p, d], self.near(p, step))

    def c_copy(self, ch, arriving=False):
        x, y, z, c = self.at
        half = 1 - c if arriving else c
        ref = self.full.at[ch, :, pl.ds(pl.multiple_of(half * HALF, 8), HALF)]
        return remote(ref, ref, self.cs.at[ch], self.cr.at[ch], device(x, y, z, 1 - c))

    def begin(self, layer):
        def send(i):
            for p in (0, 1):
                for rel in (1, 3, 2):
                    self.x_copy(layer * 6 + i, p, rel).start()

        loop(6, send)

    def advance(self, k):
        @pl.when(k < CHUNKS)
        def _():
            for p in (0, 1):
                for rel in (1, 2, 3):
                    self.x_copy(k, p, rel).wait_recv()
            for p, d in self.BOTH:
                self.a_copy(k, p, d).start()

        @pl.when((k >= 1) & (k < CHUNKS + 1))
        def _():
            for p, d in self.BOTH:
                self.a_copy(k - 1, p, d, True).wait_recv()
            for p, d in self.BOTH:
                self.b_copy(k - 1, p, d).start()

        @pl.when((k >= 2) & (k < CHUNKS + 2))
        def _():
            for p, d in self.BOTH:
                self.b_copy(k - 2, p, d, True).wait_recv()
            self.c_copy(k - 2).start()

    def arrive(self, ch):
        self.c_copy(ch, True).wait_recv()

    def end(self):
        def sent(ch):
            for p in (0, 1):
                for rel in (1, 2, 3):
                    self.x_copy(ch, p, rel).wait_send()
            for p, d in self.BOTH:
                self.a_copy(ch, p, d).wait_send()
                self.b_copy(ch, p, d).wait_send()
            self.c_copy(ch).wait_send()

        loop(CHUNKS, sent)


class Nowhere:
    end = lambda self: None
    begin = advance = arrive = lambda self, k: None


PAIR_AT = (0, 256, 384, 512)
THIRD_AT = (128, 192, 640, 704)


def repack_heads(st, wb):
    for a in range(2):
        for r in range(4):
            to, third = a * 768 + PAIR_AT[r], a * 768 + THIRD_AT[r]
            wb[to : to + 128] = st[r, a * 192 : a * 192 + 128].astype(bf)
            wb[third : third + 64] = st[r, a * 192 + 128 : a * 192 + 192].astype(bf)


def repack_hidden(st, wb):
    for a in range(3):
        for r in range(4):
            to = a * 512 + r * 128
            wb[to : to + 128] = st[r, a * 128 : a * 128 + 128].astype(bf)


def transpose_to(dst, src):
    for t in range(NB):
        dst[:, t * T : (t + 1) * T] = src[t * T : (t + 1) * T, :].T


def rms(r):
    return lax.rsqrt(jnp.mean(r * r, axis=-1, keepdims=True) + EPS)


def rope(v, cs, sl, sr):
    return v * cs + pltpu.roll(v, 96, 1) * sl + pltpu.roll(v, 32, 1) * sr


def rope_sides(sn):
    first = (lane(sn.shape) % 64) < 32
    return jnp.where(first, -sn, 0.0), jnp.where(first, 0.0, sn)


def head_lanes(h, shape):
    at = lane(shape)
    mine = at < 64 if h == 0 else at >= 64
    base = 64 if h == 0 else 0
    return mine, at - base


def project(u, wqk, wv, cs, sn, length, qa, ka, va, v, k):
    def step(t):
        at = block(t)
        ut = u[at]
        c = cs[at]
        sl, sr = rope_sides(sn[at])
        shape = (T, 128)
        bias = jnp.where(line(shape) + t * T < length, 0.0, NEG)
        val = nt(ut, wqk[0:768])
        for p in range(6):
            q_p = rope(val[:, p * 128 : p * 128 + 128], c, sl, sr)
            for h in range(2):
                mine, side = head_lanes(h, shape)
                qa[2 * p + h, at] = jnp.where(mine, q_p, jnp.where(side == 0, 1.0, 0.0)).astype(bf)
        val = nt(ut, wqk[768:1536])
        for p in range(6):
            k_p = rope(val[:, p * 128 : p * 128 + 128], c, sl, sr)
            k[p, at] = k_p.astype(bf)
            for h in range(2):
                mine, side = head_lanes(h, shape)
                other = jnp.where(side == 0, bias, jnp.where(side < 4, -1.0, 0.0))
                ka[2 * p + h, at] = jnp.where(mine, k_p, other).astype(bf)
        val = nt(ut, wv[0:768])
        for p in range(6):
            v_p = val[:, p * 128 : p * 128 + 128]
            v[p, at] = v_p.astype(bf)
            for h in range(2):
                mine, side = head_lanes(h, shape)
                va[2 * p + h, at] = jnp.where(mine, v_p, jnp.where((side >= 1) & (side < 4), -1.0, 0.0)).astype(bf)

    loop(NB, step)


def attend(qa, ka, vt, o, ob, lse, tick):
    def pair(p):
        at_l = pl.ds(pl.multiple_of(p * 128, 128), 128)
        for i in range(NB):
            n = (i + 1) * T
            rows = pl.ds(i * T, T)
            diag = line((T, T)) <= lane((T, T))
            outs, outl = [], []
            for h in range(2):
                s = nt(ka[2 * p + h, 0:n], qa[2 * p + h, rows])
                tail = jnp.where(diag, s[n - T :], NEG)
                s = tail if i == 0 else jnp.concatenate([s[: n - T], tail], axis=0)
                m = jnp.max(s, axis=0, keepdims=True) * SCALE2
                e = jnp.exp2(s * SCALE2 - m)
                tot = jnp.sum(e, axis=0, keepdims=True)
                pr = e * (1.0 / tot)
                pb = pr.astype(bf)
                main = nn(vt[p, h * 64 : h * 64 + 64, 0:n], pb)
                rest = (pr - pb.astype(f32)).astype(bf)
                outs.append(main)
                outl.append(main + nn(vt[p, h * 64 : h * 64 + 64, 0:n], rest))
                lse[pl.ds(p * 2 + h, 1), rows] = m + jnp.log2(tot)
            ob[rows, at_l] = jnp.concatenate(outs, axis=0).T.astype(bf)
            o[rows, at_l] = jnp.concatenate(outl, axis=0).T
        tick(p)

    loop(6, pair)


def three(v):
    hi = v.astype(bf).astype(f32)
    mid = (v - hi).astype(bf).astype(f32)
    low = (v - hi - mid).astype(bf).astype(f32)
    return (hi + pltpu.roll(mid, 16, 1) + pltpu.roll(low, 32, 1)).astype(bf)


def spread_table():
    table = np.zeros((128, 12 * 128), np.float32)
    for h in range(12):
        for j in range(3):
            table[16 * j + h, h * 128 + (65 if h % 2 == 0 else 1) + j] = 1.0
    return table.astype(ml_dtypes.bfloat16)


FWD_OUT = [
    ((CHUNKS, 1536, D), bf),
    ((2, 2, D, S), bf),
    ((2, 12, S, 128), bf),
    ((2, 12, S, 128), bf),
    ((2, 12, S, 128), bf),
    ((2, 6, 128, S), bf),
    ((2, S, D), f32),
    ((2, S, 256), bf),
    ((2, 4, S, 512), f32),
    ((2, 4, S, 512), f32),
    ((2, 4, S, 128), bf),
    ((4, S, D), f32),
    ((S, D), f32),
]
FWD_VMEM = [
    ((S, D), f32),
    ((2, 4, ROWS, D), f32),
    ((2, 1536, D), bf),
    ((12, S, 128), bf),
    ((12, S, 128), bf),
    ((12, S, 128), bf),
    ((6, S, 128), bf),
    ((6, S, 128), bf),
    ((6, 128, S), bf),
    ((6, 128, S), bf),
    ((S, D), f32),
    ((S, D), bf),
    ((128, S), f32),
    ((S, D), bf),
    ((2, D, S), bf),
    ((S, D), f32),
    ((S, D), f32),
    ((2, 2, 512, 512), f32),
    ((4, S, 128), bf),
    ((3, 192, D), bf),
    ((192, D), bf),
    ((2, D, 512), bf),
    ((512, D), bf),
]


def fwd_kernel(comm, length_ref, wq, wk, wv, wo, wg, wu, wd, x_hbm, cs, sn, gains, spread, *rest):
    own, full, rest = (rest[1], rest[0], rest[2:]) if not comm else (rest[0], rest[1], rest[2:])
    outs, rest = rest[: len(FWD_OUT)], rest[len(FWD_OUT) :]
    w_o, ut_o, qa_o, ka_o, va_o, kt_o, o_o, ob_o, a_o, b_o, hb_o, res_o, out_o = outs
    (x, st, wb, qa, ka, va, k, v, kt, vt, o, ob, lse, u, ut, acc, res, ab, hb, raw_h, raw_o, raw_f, raw_d), rest = (
        rest[: len(FWD_VMEM)],
        rest[len(FWD_VMEM) :],
    )
    load_sem, w_sem, save_sem, ab_sem, own_sem = rest[:5]
    net = Gather(own, full, rest[5:]) if comm else Nowhere()
    length = length_ref[0]

    def raw(layer):
        places = (raw_h.at[0], raw_h.at[1], raw_h.at[2], raw_o, raw_f.at[0], raw_f.at[1], raw_d)
        return [
            pltpu.make_async_copy(src.at[layer], dst, own_sem.at[i])
            for i, (src, dst) in enumerate(zip((wq, wk, wv, wo, wg, wu, wd), places))
        ]

    def own_chunks(layer):
        if layer == 0:
            return [st.at[i // 4, i % 4] for i in range(6)]
        return [st.at[1, 2], st.at[1, 3]] + [b.at[pl.ds(i * ROWS, ROWS)] for b in (acc, res) for i in range(2)]

    def own_puts(layer):
        return [
            pltpu.make_async_copy(src, own.at[layer * 6 + i], own_sem.at[i])
            for i, src in enumerate(own_chunks(layer))
        ]

    def turn(dst, row, src):
        for t in range(3):
            dst[row : row + src.shape[1], t * T : (t + 1) * T] = src[t * T : (t + 1) * T, :].astype(f32).T

    def prepare(layer):
        to = own_chunks(layer)
        for copy in raw(layer):
            copy.wait()
        for i in range(3):
            to[i // 2][i % 2 * 192 : i % 2 * 192 + 192] = raw_h[i].astype(f32)
        to[1][192:384] = raw_o[...].astype(f32)
        for f in range(4):
            for i in range(2):
                turn(to[2 + f], i * 128, raw_f.at[i, :, pl.ds(f * 128, 128)])
            to[2 + f][256:384] = raw_d[f * 128 : f * 128 + 128].astype(f32)
        for copy in own_puts(layer):
            copy.start()

    for copy in raw(0):
        copy.start()
    x_in = pltpu.make_async_copy(x_hbm, x, save_sem.at[0])
    x_in.start()
    prepare(0)
    if comm:
        greet()
    for copy in own_puts(0):
        copy.wait()
    net.begin(0)
    for copy in raw(1):
        copy.start()
    prepare(1)
    for copy in own_puts(1):
        copy.wait()
    net.begin(1)
    x_in.wait()

    def loads(ch, slot):
        return (
            pltpu.make_async_copy(own.at[ch], st.at[slot, 0], load_sem.at[slot, 0]),
            pltpu.make_async_copy(full.at[ch], st.at[slot, pl.ds(1, 3)], load_sem.at[slot, 1]),
        )

    def start_load(ch, slot):
        net.arrive(ch)
        for copy in loads(ch, slot):
            copy.start()

    def put_weights(ch, slot):
        return pltpu.make_async_copy(wb.at[slot], w_o.at[ch], w_sem.at[slot])

    def unpack(ch, slot, repack, first=False):
        for copy in loads(ch, slot):
            copy.wait()
        if not first:
            put_weights(ch, slot).wait()
        repack(st.at[slot], wb.at[slot])
        put_weights(ch, slot).start()

    flying = {}

    def save(name, src, dst, i):
        flying[name] = pltpu.make_async_copy(src, dst, save_sem.at[i])
        flying[name].start()

    def settle(*names):
        for name in names:
            if name in flying:
                flying.pop(name).wait()

    loop(4, net.advance)
    start_load(0, 0)
    start_load(1, 1)
    lse[...] = jnp.zeros((128, S), f32)
    for layer in range(2):
        base = layer * 6
        settle("uta")
        net.advance(base + 4 if layer == 0 else 11)

        def enter(t):
            at = block(t)
            val = x[at]
            if layer:
                val = val * rms(val) * gains[2:3]
            u[at] = val.astype(bf)

        loop(NB, enter)
        transpose_to(ut.at[0], u)
        save("uta", ut.at[0], ut_o.at[layer, 0], 0)
        unpack(base, 0, repack_heads, layer == 0)
        unpack(base + 1, 1, repack_heads, layer == 0)
        start_load(base + 2, 0)
        settle("qa", "ka", "va", "kt", "o", "ob")
        project(u, wb.at[0], wb.at[1], cs, sn, length, qa, ka, va, v, k)
        for p in range(6):
            transpose_to(kt.at[p], k.at[p])
            transpose_to(vt.at[p], v.at[p])
        save("ka", ka, ka_o.at[layer], 1)
        save("va", va, va_o.at[layer], 2)
        save("kt", kt, kt_o.at[layer], 3)
        net.advance(5 if layer == 0 else 12)

        def tick(p):
            @pl.when(lax.rem(p, 2) == 1)
            def _():
                net.advance((6 if layer == 0 else 13) + p // 2)

        attend(qa, ka, vt, o, ob, lse, tick)
        save("o", o, o_o.at[layer], 4)
        save("ob", ob.at[:, pl.ds(0, 256)], ob_o.at[layer], 5)

        def add_lse(t):
            at = block(t)
            val = nn(three(lse[:, at].T * (1.0 / SCALE2)), spread[...])
            for h in range(12):
                qa[h, at] = (qa[h, at].astype(f32) + val[:, h * 128 : h * 128 + 128]).astype(bf)

        loop(NB, add_lse)
        save("qa", qa, qa_o.at[layer], 6)
        settle("res")

        def after(t):
            at = block(t)
            r = x[at] + nn(ob[at], wb[1, 768:1536])
            res[at] = r
            n = r * rms(r)
            if layer == 0:
                h = n * gains[0:1]
                acc[at] = h
                u[at] = h.astype(bf)
            else:
                acc[at] = r
                u[at] = (n * gains[3:4]).astype(bf)

        loop(NB, after)
        save("res", res, res_o.at[2 * layer if layer == 0 else 3], 7)
        settle("utf")
        transpose_to(ut.at[1], u)
        save("utf", ut.at[1], ut_o.at[layer, 1], 8)
        settle("hb")

        def chunk(f):
            ch = base + 2 + f
            slot = lax.rem(f, 2)

            @pl.when(ch + 1 < CHUNKS)
            def _():
                start_load(ch + 1, 1 - slot)

            if layer == 0:

                @pl.when(lax.rem(f, 2) == 0)
                def _():
                    net.advance(9 + f // 2)

            unpack(ch, slot, repack_hidden)
            w = wb.at[slot]

            def step(t):
                at = block(t, 512)

                def put(j):
                    return pltpu.make_async_copy(ab.at[t, j], (a_o, b_o)[j].at[layer, f, at], ab_sem.at[t, j])

                @pl.when(f >= 1)
                def _():
                    put(0).wait()
                    put(1).wait()

                ub = u[at]
                gate = nt(ub, w[0:512])
                up = nt(ub, w[512:1024])
                sig = 1.0 / (1.0 + jnp.exp(-gate))
                a = gate * sig
                hid = (a * up).astype(bf)
                ab[t, 0] = a
                ab[t, 1] = up * (sig + a * (1.0 - sig))
                hb[f, at] = hid[:, 0:128]
                acc[at] = acc[at] + nn(hid, w[1024:1536])
                put(0).start()
                put(1).start()

            loop(2, step)

        loop(4, chunk)
        for t in range(2):
            for j in range(2):
                pltpu.make_async_copy(ab.at[t, j], a_o.at[layer, 0, block(0, 512)], ab_sem.at[t, j]).wait()
        save("hb", hb, hb_o.at[layer], 9)
        if layer == 0:
            start_load(7, 1)
            settle("res")

            def leave(t):
                at = block(t)
                r = acc[at]
                res[at] = r
                x[at] = r * rms(r) * gains[1:2]

            loop(NB, leave)
            save("res", res, res_o.at[1], 7)
            save("y", x, res_o.at[2], 10)
        else:
            settle("y")

            def last(t):
                at = block(t)
                x[at] = jnp.where(line((T, 1)) + t * T < length, acc[at], 0.0)

            loop(NB, last)
            save("out", x, out_o, 11)
    settle(*list(flying))
    for slot in range(2):
        put_weights(0, slot).wait()
    net.end()


def whole(memory):
    return pl.BlockSpec(memory_space=memory)


def forward(length, weights, x, cs, sn, gains, spread, full=None):
    comm = full is None
    hbm, vmem = whole(pl.ANY), whole(pltpu.VMEM)
    extra = [((CHUNKS, ROWS, D), f32)] + ([((CHUNKS, 3, ROWS, D), f32)] if comm else [])
    outs = [jax.ShapeDtypeStruct(s, d) for s, d in extra + FWD_OUT]
    dma = pltpu.SemaphoreType.DMA
    result = pl.pallas_call(
        lambda *refs: fwd_kernel(comm, *refs),
        out_shape=outs,
        in_specs=[whole(pltpu.SMEM)] + [hbm] * 8 + [vmem] * 4 + ([] if comm else [hbm]),
        out_specs=[hbm] * len(outs),
        scratch_shapes=[pltpu.VMEM(s, d) for s, d in FWD_VMEM]
        + [dma((2, 2)), dma((2,)), dma((12,)), dma((2, 2)), dma((7,))]
        + ([dma(s) for s in Gather.SEMS] if comm else []),
        compiler_params=pltpu.CompilerParams(
            vmem_limit_bytes=63 * 2**20,
            **(dict(collective_id=0, has_side_effects=True) if comm else {}),
        ),
    )(length, *weights, x, cs, sn, gains, spread, *([] if comm else [full]))
    return result[len(extra) :]


GROUPS = 6
GRAD_ROWS = 24


class Scatter:
    SEMS = [(GROUPS,)] * 2 + [(GROUPS, 2, 3)] * 4 + [(7,)] * 2
    VMEM = [
        ((2, 2, 16, GRAD_ROWS, D), f32),
        ((4, 16, GRAD_ROWS, D), f32),
        ((2, 2, 3, 4, GRAD_ROWS, D // 2), f32),
        ((2, 2, 3, GRAD_ROWS, D // 2), f32),
        ((8, D), f32),
        ((7, 8, D), f32),
    ]

    def __init__(self, out, bufs, sems):
        self.out = out
        self.grads, self.sums, self.one, self.two, self.gain, self.gains_in = bufs
        self.cs, self.cr, self.s1, self.r1, self.s2, self.r2, self.gs, self.gr = sems
        self.at = place()

    def peer(self, along, k):
        x, y, z, c = self.at
        return device(x, y + k, z, c) if along == 0 else device(x, y, z + k, c)

    def greet(self):
        x, y, z, c = self.at
        bar = pltpu.get_barrier_semaphore()
        to = [self.peer(a, k) for a in (0, 1) for k in (1, 2, 3)] + [device(x, y, z, 1 - c)]
        for other in to:
            pl.semaphore_signal(bar, inc=1, device_id=other, device_id_type=MESH)
        pl.semaphore_wait(bar, 7)

    def columns(self, part):
        return pl.ds(part * (D // 2), D // 2)

    def core_copy(self, g):
        x, y, z, c = self.at
        return remote(
            self.grads.at[lax.rem(g, 2), 1 - c],
            self.sums.at[lax.rem(g, 4)],
            self.cs.at[g],
            self.cr.at[g],
            device(x, y, z, 1 - c),
        )

    def four(self, g, part, pos):
        ref = self.sums.at[lax.rem(g, 4)]
        if part == 0:
            return ref.at[pl.ds(pos * 4, 4), :, self.columns(0)]
        return ref

    def one_copies(self, g, part, k):
        pos = lax.rem(self.at[1 + part] + k, 4)
        slot = lax.rem(g, 2)
        dst = self.one.at[slot, part, 3 - k]
        send, recv, to = self.s1.at[g, part, k - 1], self.r1.at[g, part, 3 - k], self.peer(part, k)
        sums = self.sums.at[lax.rem(g, 4)]
        if part == 0:
            return [remote(sums.at[pl.ds(pos * 4, 4), :, self.columns(0)], dst, send, recv, to)]
        return [remote(sums.at[i * 4 + pos, :, self.columns(1)], dst.at[i], send, recv, to) for i in range(4)]

    def one_wait(self, g, part, k):
        dst = self.one.at[lax.rem(g, 2), part, k - 1]
        return remote(dst, dst, self.s1.at[g, part, k - 1], self.r1.at[g, part, k - 1], self.peer(part, k))

    def two_copy(self, g, part, k):
        along = 1 - part
        pos = lax.rem(self.at[1 + along] + k, 4)
        _, y, z, _ = self.at
        index = y * 4 + pos if part == 0 else pos * 4 + z
        return remote(
            self.sums.at[lax.rem(g, 4), index, :, self.columns(part)],
            self.two.at[lax.rem(g, 2), part, 3 - k],
            self.s2.at[g, part, k - 1],
            self.r2.at[g, part, 3 - k],
            self.peer(along, k),
        )

    def two_wait(self, g, part, k):
        dst = self.two.at[lax.rem(g, 2), part, k - 1]
        return remote(dst, dst, self.s2.at[g, part, k - 1], self.r2.at[g, part, k - 1], self.peer(1 - part, k))

    def gain_copy(self, step, k=0):
        x, y, z, c = self.at
        if step == 0:
            i = j = 0
            to = device(x, y, z, 1 - c)
        else:
            i, j = 3 * step - 3 + k, 3 * step - 3 + 4 - k
            to = self.peer(step - 1, k)
        return remote(self.gain, self.gains_in.at[j], self.gs.at[i], self.gr.at[j], to)

    def stage0(self, g):
        self.core_copy(g).start()

    def stage1(self, g):
        copy = self.core_copy(g)
        copy.wait_recv()
        c = self.at[3]
        slot, ring = lax.rem(g, 2), lax.rem(g, 4)

        def add(i):
            self.sums[ring, i] = self.sums[ring, i] + self.grads[slot, c, i]

        loop(16, add)
        for part in (0, 1):
            for k in (1, 3, 2):
                for one in self.one_copies(g, part, k):
                    one.start()
        copy.wait_send()

    def stage2(self, g):
        for part in (0, 1):
            for k in (1, 2, 3):
                self.one_wait(g, part, k).wait_recv()
        _, y, z, _ = self.at
        slot, ring = lax.rem(g, 2), lax.rem(g, 4)

        def add(i):
            for part in (0, 1):
                at = (y * 4 + i) if part == 0 else (i * 4 + z)
                cols = pl.ds(part * (D // 2), D // 2)
                got = self.one[slot, part, 0, i] + self.one[slot, part, 1, i] + self.one[slot, part, 2, i]
                self.sums[ring, at, :, cols] = self.sums[ring, at, :, cols] + got

        for part in (0, 1):
            for k in (1, 2, 3):
                self.one_sent(g, part, k)
        loop(4, add)
        for part in (0, 1):
            for k in (1, 3, 2):
                self.two_copy(g, part, k).start()

    def one_sent(self, g, part, k):
        for one in self.one_copies(g, part, k):
            one.wait_send()

    def stage3(self, g):
        for part in (0, 1):
            for k in (1, 2, 3):
                self.two_wait(g, part, k).wait_recv()
        _, y, z, _ = self.at
        slot, ring = lax.rem(g, 2), lax.rem(g, 4)
        for part in (0, 1):
            cols = pl.ds(part * (D // 2), D // 2)
            got = self.two[slot, part, 0] + self.two[slot, part, 1] + self.two[slot, part, 2]
            self.out[g, :, cols] = self.sums[ring, y * 4 + z, :, cols] + got
        for part in (0, 1):
            for k in (1, 2, 3):
                self.two_copy(g, part, k).wait_send()

    def tick(self, n):
        @pl.when((n >= 3) & (n < GROUPS + 3))
        def _():
            self.stage3(n - 3)

        @pl.when((n >= 2) & (n < GROUPS + 2))
        def _():
            self.stage2(n - 2)

        @pl.when((n >= 1) & (n < GROUPS + 1))
        def _():
            self.stage1(n - 1)

        @pl.when(n < GROUPS)
        def _():
            self.stage0(n)

    def gain_start(self, step):
        if step == 0:
            self.gain_copy(0).start()
        else:
            for k in (1, 2, 3):
                self.gain_copy(step, k).start()

    def gain_finish(self, step):
        copies = [self.gain_copy(0)] if step == 0 else [self.gain_copy(step, k) for k in (1, 2, 3)]
        for copy in copies:
            copy.wait()
        first = 0 if step == 0 else 3 * step - 2
        for j in range(first, first + len(copies)):
            self.gain[...] = self.gain[...] + self.gains_in[j]


class Keep:
    VMEM = Scatter.VMEM

    def __init__(self, out, bufs, sems):
        self.out, self.grads, self.gain, self.sem = out, bufs[0], bufs[4], sems[0]

    def greet(self):
        pass

    def tick(self, n):
        @pl.when(n < GROUPS)
        def _():
            copy = pltpu.make_async_copy(self.grads.at[lax.rem(n, 2)], self.out.at[n], self.sem)
            copy.start()
            copy.wait()

    def gain_start(self, step):
        pass

    gain_finish = gain_start


BWD_VMEM = [
    ((S, D), f32),
    ((S, D), f32),
    ((S, D), f32),
    ((S, D), bf),
    ((D, S), bf),
    ((D, S), bf),
    ((2, 1536, D), bf),
    ((2, 2, 512, 512), f32),
    ((12, S, 128), bf),
    ((12, S, 128), bf),
    ((12, S, 128), bf),
    ((12, S, 128), bf),
    ((6, 128, S), bf),
    ((S, D), bf),
    ((S, D), bf),
    ((S, D), bf),
    ((128, S), f32),
    ((4, S, 256), bf),
]


def bwd_kernel(comm, length_ref, cot, w, uts, qas, kas, vas, kts, os_, obs, as_, bs, hbs, ress, cs, sn, gains, spread, *rest):
    input_grad, gain_out, grad_out = rest[:3]
    rest = rest[3:]
    (e, acc, res, eb, ebt, ut, wb, ab, qa, ka, va, da, kt, dq, dk, dv, dqt, own), rest = (
        rest[: len(BWD_VMEM)],
        rest[len(BWD_VMEM) :],
    )
    bufs, rest = rest[: len(Scatter.VMEM)], rest[len(Scatter.VMEM) :]
    load_sem, w_sem, ab_sem, rest = rest[0], rest[1], rest[2], rest[3:]
    net = (Scatter if comm else Keep)(grad_out, bufs, rest)
    grads, gain = bufs[0], bufs[4]
    length = length_ref[0]

    flying = {}

    def fetch(name, src, dst, i):
        flying[name] = pltpu.make_async_copy(src, dst, load_sem.at[i])
        flying[name].start()

    def need(*names):
        for name in names:
            flying.pop(name).wait()

    def weights(ch, slot):
        return pltpu.make_async_copy(w.at[ch], wb.at[slot], w_sem.at[slot])

    def factors(layer, f, t):
        return [
            pltpu.make_async_copy(src.at[layer, f, block(t, 512)], ab.at[t, j], ab_sem.at[t, j])
            for j, src in ((0, as_), (1, bs))
        ]

    def round_grad():
        def step(t):
            at = block(t)
            eb[at] = e[at].astype(bf)

        loop(NB, step)
        transpose_to(ebt, eb)

    def norm_back(incoming, r, row):
        fac = rms(r)
        n = r * fac
        gain[row : row + 1] = gain[row : row + 1] + jnp.sum(incoming * n, axis=0, keepdims=True)
        inner = incoming * gains[row : row + 1]
        return fac * (inner - n * jnp.mean(inner * n, axis=-1, keepdims=True))

    def outer(slot, cols, left, right):
        def step(i):
            val = nn(left[block(i, 192)], right())
            for b in range(8):
                grads[slot, b % 2, i * 4 + b // 2, :, cols] = val[b * 24 : b * 24 + 24]

        loop(4, step)

    gain[...] = jnp.zeros((8, D), f32)
    fetch("cot", cot, e, 0)
    fetch("ut", uts.at[1, 1], ut, 1)
    fetch("res", ress.at[3], res, 2)
    weights(8, 0).start()
    for t in range(2):
        for copy in factors(1, 0, t):
            copy.start()
    net.greet()
    need("cot")

    def mask(t):
        at = block(t)
        e[at] = jnp.where(line((T, 1)) + t * T < length, e[at], 0.0)

    loop(NB, mask)

    for layer in (1, 0):
        base = layer * 6
        group = 3 * (1 - layer)
        round_grad()

        def clear(t):
            acc[block(t)] = jnp.zeros((T, D), f32)

        loop(NB, clear)
        need("ut")

        def half(hh):
            for i in range(2):
                pltpu.make_async_copy(
                    hbs.at[layer, 2 * hh + i], own.at[2, :, pl.ds(i * 128, 128)], load_sem.at[8 + i]
                ).start()

            for i in range(2):
                f = 2 * hh + i
                ch = base + 2 + f
                weights(ch, i).wait()
                if i == 0:
                    weights(ch + 1, 1).start()
                else:

                    @pl.when(hh == 0)
                    def _():
                        weights(ch + 1, 0).start()

                    @pl.when(hh == 1)
                    def _():
                        weights(base, 0).start()

                def step(t):
                    at = block(t, 512)
                    for copy in factors(layer, f, t):
                        copy.wait()
                    a, b = ab[t, 0], ab[t, 1]
                    dh = nt(eb[at], wb[i, 1024:1536])
                    dg = (dh * b).astype(bf)
                    du = (dh * a).astype(bf)
                    own[0, at, i * 128 : i * 128 + 128] = dg[:, 0:128]
                    own[1, at, i * 128 : i * 128 + 128] = du[:, 0:128]
                    acc[at] = acc[at] + nn(dg, wb[i, 0:512]) + nn(du, wb[i, 512:1024])

                    @pl.when(f < 3)
                    def _():
                        for copy in factors(layer, f + 1, t):
                            copy.start()

                loop(2, step)
            for i in range(2):
                pltpu.make_async_copy(
                    hbs.at[layer, 2 * hh + i], own.at[2, :, pl.ds(i * 128, 128)], load_sem.at[8 + i]
                ).wait()
            slot = lax.rem(group + hh, 2)
            outer(slot, pl.ds(0, 256), ut, lambda: own[0])
            outer(slot, pl.ds(256, 256), ut, lambda: own[1])
            outer(slot, pl.ds(512, 256), ebt, lambda: own[2])
            net.tick(group + hh)

        loop(2, half)
        weights(base + 1, 1).start()
        fetch("ut", uts.at[layer, 0], ut, 1)
        for i, (name, src, dst) in enumerate((("qa", qas, qa), ("ka", kas, ka), ("va", vas, va), ("kt", kts, kt))):
            fetch(name, src.at[layer], dst, 3 + i)
        fetch("ob", obs.at[layer], own.at[3], 7)
        need("res")

        def through(t):
            at = block(t)
            if layer:
                e[at] = e[at] + norm_back(acc[at], res[at], 3)
            else:
                e[at] = norm_back(e[at] + acc[at], res[at], 0)

        loop(NB, through)
        fetch("o", os_.at[layer], res, 2)
        round_grad()
        if layer == 0:
            net.gain_start(0)
        weights(base, 0).wait()
        weights(base + 1, 1).wait()
        need("o")
        owner = jnp.where(line((D, 128)) // 64 == lane((D, 128)), 1.0, 0.0).astype(bf)

        def mixed_back(t):
            at = block(t)
            val = nt(eb[at], wb[1, 768:1536]).astype(bf)
            prod = val.astype(f32) * res[at]
            hi = prod.astype(bf)
            low = (prod - hi.astype(f32)).astype(bf)
            inner = nn(three(nn(hi, owner) + nn(low, owner)), spread[...])
            for h in range(12):
                mine, _ = head_lanes(h % 2, (T, 128))
                pair = val[:, (h // 2) * 128 : (h // 2) * 128 + 128]
                da[h, at] = jnp.where(mine, pair, inner[:, h * 128 : h * 128 + 128].astype(bf))

        loop(NB, mixed_back)
        if layer:
            fetch("res", ress.at[2], res, 2)
        need("qa", "ka", "va", "kt", "ut", "ob")
        low = lane((T, 128)) < 64

        def pair(p):
            at_l = pl.ds(pl.multiple_of(p * 128, 128), 128)
            for j in range(NB):
                ks, qs = pl.ds(j * T, T), pl.ds(j * T, S - j * T)
                diag = line((T, T)) <= lane((T, T))
                dvs, dks = [], []
                for h in range(2):
                    hd = 2 * p + h
                    s = nt(ka[hd, ks], qa[hd, qs])
                    dp = nt(va[hd, ks], da[hd, qs])
                    pr = jnp.exp2(s * SCALE2)
                    head = jnp.where(diag, pr[:, :T], 0.0)
                    pr = head if j == NB - 1 else jnp.concatenate([head, pr[:, T:]], axis=1)
                    ds = (pr * dp).astype(bf)
                    dvs.append(nn(pr.astype(bf), da[hd, qs]))
                    dks.append(nn(ds, qa[hd, qs]))
                    val = nn(kt[p, h * 64 : h * 64 + 64, ks], ds)
                    if j == 0:
                        dqt[h * 64 : h * 64 + 64, :] = val
                    else:
                        dqt[h * 64 : h * 64 + 64, j * T :] = dqt[h * 64 : h * 64 + 64, j * T :] + val
                dv[ks, at_l] = jnp.where(low, dvs[0], dvs[1]).astype(bf)
                sl, sr = rope_sides(sn[ks])
                dk_j = jnp.where(low, dks[0], dks[1]) * 0.125
                dk[ks, at_l] = rope(dk_j, cs[ks], -sl, -sr).astype(bf)
            for j in range(NB):
                ks = pl.ds(j * T, T)
                sl, sr = rope_sides(sn[ks])
                dq_j = dqt[:, j * T : j * T + T].T * 0.125
                dq[ks, at_l] = rope(dq_j, cs[ks], -sl, -sr).astype(bf)

        loop(2, pair)
        slot = (group + 2) % 2

        def own_heads(i):
            at = block(i, 192)
            vals = [nn(ut[at], dq[:, 0:256]), nn(ut[at], dk[:, 0:256]), nn(ut[at], dv[:, 0:256]), nn(ebt[at], own[3])]
            left = lane((192, 128)) < 64
            tiles = [v[:, 0:128] for v in vals] + [
                jnp.where(left, vals[n][:, 128:256], pltpu.roll(vals[n + 1][:, 128:256], 64, 1)) for n in (0, 2)
            ]
            for n, tile in enumerate(tiles):
                for b in range(8):
                    grads[slot, b % 2, i * 4 + b // 2, :, n * 128 : n * 128 + 128] = tile[b * 24 : b * 24 + 24]

        loop(4, own_heads)
        net.tick(group + 2)
        if layer:
            fetch("ut", uts.at[0, 1], ut, 1)
            loop(4, lambda p: pair(p + 2))
        else:
            net.gain_finish(0)
            net.gain_start(1)
            loop(2, lambda p: pair(p + 2))
            net.tick(6)
            net.gain_finish(1)
            net.gain_start(2)
            loop(2, lambda p: pair(p + 4))
            net.tick(7)
            net.gain_finish(2)

        def into(t):
            at = block(t)
            val = nn(dq[at], wb[0, 0:768]) + nn(dk[at], wb[0, 768:1536]) + nn(dv[at], wb[1, 0:768])
            acc[at] = val

        loop(NB, into)
        if layer:
            weights(2, 0).start()
            for t in range(2):
                for copy in factors(0, 0, t):
                    copy.start()
            need("res")

            def between(t):
                at = block(t)
                e[at] = e[at] + norm_back(acc[at], res[at], 2)

            loop(NB, between)
            fetch("res", ress.at[1], res, 2)
            need("res")

            def below(t):
                at = block(t)
                e[at] = norm_back(e[at], res[at], 1)

            loop(NB, below)
            fetch("res", ress.at[0], res, 2)
        else:

            def last(t):
                at = block(t)
                acc[at] = e[at] + acc[at]

            loop(NB, last)
            done = pltpu.make_async_copy(acc, input_grad, load_sem.at[0])
            done.start()
            gain_out[...] = gain[...]
            net.tick(8)
            done.wait()


def backward(comm, length, cot, kept, cs, sn, gains, spread):
    hbm, vmem = whole(pl.ANY), whole(pltpu.VMEM)
    dma = pltpu.SemaphoreType.DMA
    w, uts, qas, kas, vas, kts, os_, obs, as_, bs, hbs, ress = kept[:12]
    grad = (GROUPS, GRAD_ROWS, D) if comm else (GROUPS, 2, 16, GRAD_ROWS, D)
    return pl.pallas_call(
        lambda *refs: bwd_kernel(comm, *refs),
        out_shape=[jax.ShapeDtypeStruct(s, f32) for s in [(S, D), (8, D), grad]],
        in_specs=[whole(pltpu.SMEM)] + [hbm] * 13 + [vmem] * 4,
        out_specs=[hbm, vmem, vmem if comm else hbm],
        scratch_shapes=[pltpu.VMEM(s, d) for s, d in BWD_VMEM + Scatter.VMEM]
        + [dma((10,)), dma((2,)), dma((2, 2))]
        + ([dma(s) for s in Scatter.SEMS] if comm else [dma]),
        compiler_params=pltpu.CompilerParams(
            vmem_limit_bytes=63 * 2**20,
            **(dict(collective_id=1, has_side_effects=True) if comm else {}),
        ),
    )(length, cot, w, uts, qas, kas, vas, kts, os_, obs, as_, bs, hbs, ress, cs, sn, gains, spread)


def finish_kernel(out_in, grad_in, sums, gain, out, grad, q, k, v, o, gate, up, down, gains, last, big, sem):
    parts = [(src, dst, t) for src, dst in ((out_in, out), (grad_in, grad)) for t in range(NB)]

    def get(n):
        src, _, t = parts[n]
        return pltpu.make_async_copy(src.at[pl.ds(t * T, T)], big.at[n], sem.at[n])

    def put(n):
        _, dst, t = parts[n]
        return pltpu.make_async_copy(big.at[n], dst.at[pl.ds(t * T, T)], sem.at[n])

    for n in range(len(parts)):
        get(n).start()
    for layer in range(2):
        heads = sums.at[5 - 3 * layer]
        thirds = [heads[:, 512:640], heads[:, 640:768]]
        thirds = [thirds[0], pltpu.roll(thirds[0], 64, 1), thirds[1], pltpu.roll(thirds[1], 64, 1)]
        for n, to in enumerate((q, k, v, o)):
            to[layer, :, 0:128] = heads[:, n * 128 : n * 128 + 128]
            to[layer, :, 128:192] = thirds[n][:, 0:64]
        for half in range(2):
            for n, to in enumerate((gate, up, down)):
                to[layer, :, half * 256 : half * 256 + 256] = sums[3 - 3 * layer + half, :, n * 256 : n * 256 + 256]
    mine = pltpu.roll(gain[...], lax.rem(D - lax.axis_index("dp") * GRAD_ROWS, D), 1)
    gains[...] = mine[0:3, 0:GRAD_ROWS]
    last[...] = mine[3:4, 0:GRAD_ROWS]
    for n in range(len(parts)):
        get(n).wait()
        put(n).start()
    for n in range(len(parts)):
        put(n).wait()


def finish(out, grad, sums, gain):
    hbm, vmem = whole(pl.ANY), whole(pltpu.VMEM)
    shapes = [(S, D)] * 2 + [(2, GRAD_ROWS, 192)] * 4 + [(2, GRAD_ROWS, 512)] * 3 + [(3, GRAD_ROWS), (1, GRAD_ROWS)]
    return pl.pallas_call(
        finish_kernel,
        out_shape=[jax.ShapeDtypeStruct(s, f32) for s in shapes],
        in_specs=[hbm, hbm, vmem, vmem],
        out_specs=[hbm, hbm] + [vmem] * 9,
        scratch_shapes=[pltpu.VMEM((2 * NB, T, D), f32), pltpu.SemaphoreType.DMA((2 * NB,))],
        compiler_params=pltpu.CompilerParams(vmem_limit_bytes=60 * 2**20),
    )(out, grad, sums, gain)


def rope_tables():
    freq = (10000.0 ** (-np.arange(32) * 2.0 / 64)).astype(np.float32)
    angle = (np.arange(S, dtype=np.float32)[:, None] * freq[None, :]).astype(np.float64)
    return tuple(np.tile(v.astype(np.float32), (1, 4)) for v in (np.cos(angle), np.sin(angle)))


def local(block_input, lengths, cotangent, w_query, w_key, w_value, w_output, w_gate, w_up, w_down, gains):
    cs, sn = rope_tables()
    spread = spread_table()
    heads = [jnp.swapaxes(w, 1, 2) for w in (w_query, w_key, w_value)]
    weights = (*heads, w_output, w_gate, w_up, w_down)
    kept = forward(lengths, weights, block_input, cs, sn, gains, spread)
    input_grad, gain_sums, grads = backward(True, lengths, cotangent, kept, cs, sn, gains, spread)
    out, input_grad, q, k, v, o, gate, up, down, gain_grads, last = finish(kept[12], input_grad, grads, gain_sums)
    return (out, input_grad, q, k, v, jnp.swapaxes(o, 1, 2), gate, up, jnp.swapaxes(down, 1, 2), gain_grads, last[0])


def solution(mesh):
    rows, cols, deep = P("dp", None), P(None, None, "tensor"), P(None, "tensor", None)
    return jax.shard_map(
        local,
        mesh=mesh,
        in_specs=(rows, P("dp"), rows, cols, cols, cols, deep, cols, cols, deep, P()),
        out_specs=(rows, rows)
        + (P(None, "dp", "tensor"),) * 3
        + (P(None, "tensor", "dp"),)
        + (P(None, "dp", "tensor"),) * 2
        + (P(None, "tensor", "dp"), P(None, "dp"), P("dp")),
        check_vma=False,
    )
```

```python
import math

import jax
import jax.numpy as jnp
import ml_dtypes
import numpy as np
from jax import lax
from jax.experimental import pallas as pl
from jax.experimental.pallas import tpu as pltpu
from jax.sharding import PartitionSpec as P

bf, f32 = jnp.bfloat16, jnp.float32
MESH = pl.DeviceIdType.MESH

CHUNKS, ROWS, D, S, T = 12, 384, 768, 1024, 256
NB = S // T
HALF, QUART, PIECE = ROWS // 2, ROWS // 4, ROWS // 16
UNIT = 128 * 4
SCALE2 = 0.125 * math.log2(math.e)
EPS = 1e-5
NEG = -1e30


def nt(a, b):
    return lax.dot_general(a, b, (((1,), (1,)), ((), ())), preferred_element_type=f32)


def nn(a, b):
    return lax.dot_general(a, b, (((1,), (0,)), ((), ())), preferred_element_type=f32)


def lane(shape):
    return lax.broadcasted_iota(jnp.int32, shape, len(shape) - 1)


def line(shape):
    return lax.broadcasted_iota(jnp.int32, shape, len(shape) - 2)


def loop(count, body):
    lax.fori_loop(0, count, lambda i, c: (body(i), c)[1], 0)


def block(t, size=T):
    return pl.ds(pl.multiple_of(t * size, size), size)


def place():
    d = lax.axis_index("dp")
    return lax.axis_index("tensor"), d // 8, (d // 2) % 4, d % 2


def device(x, y, z, c):
    return (((y % 4) * 4 + (z % 4)) * 2 + c, x % 4)


def remote(src, dst, send, recv, to):
    return pltpu.make_async_remote_copy(
        src_ref=src, dst_ref=dst, send_sem=send, recv_sem=recv, device_id=to, device_id_type=MESH
    )


def greet():
    x, y, z, c = place()
    bar = pltpu.get_barrier_semaphore()
    for to in (
        device(x + 1, y, z, c),
        device(x + 2, y, z, c),
        device(x + 3, y, z, c),
        device(x, y + 1, z, c),
        device(x, y + 3, z, c),
        device(x, y, z + 1, c),
        device(x, y, z + 3, c),
        device(x, y, z, 1 - c),
    ):
        pl.semaphore_signal(bar, inc=1, device_id=to, device_id_type=MESH)


def greeted():
    pl.semaphore_wait(pltpu.get_barrier_semaphore(), 8)


class Gather:
    SEMS = [(CHUNKS, 2, 3)] * 2 + [(CHUNKS, 2, 2)] * 4 + [(CHUNKS,)] * 2
    BOTH = [(p, d) for p in (0, 1) for d in (0, 1)]

    def __init__(self, own, full, sems):
        self.own, self.full = own, full
        self.xs, self.xr, self.as_, self.ar, self.bs, self.br, self.cs, self.cr = sems
        self.at = place()

    def rows(self, p, pos):
        c = self.at[3]
        return pl.ds(pl.multiple_of(c * HALF + p * QUART + ((pos + 4) % 4) * PIECE, 8), PIECE)

    def near(self, p, step):
        x, y, z, c = self.at
        return device(x, y + 4 + step, z, c) if p == 0 else device(x, y, z + 4 + step, c)

    def x_copy(self, ch, p, rel):
        x, y, z, c = self.at
        here = self.rows(p, self.at[1 + p])
        return remote(
            self.own.at[ch, here],
            self.full.at[ch, rel - 1, here],
            self.xs.at[ch, p, rel - 1],
            self.xr.at[ch, p, rel - 1],
            device(x + 4 - rel, y, z, c),
        )

    def a_copy(self, ch, p, d, arriving=False):
        step = 1 - 2 * d
        pos = self.at[1 + p] - step if arriving else self.at[1 + p]
        ref = self.full.at[ch, :, self.rows(p, pos)]
        return remote(ref, ref, self.as_.at[ch, p, d], self.ar.at[ch, p, d], self.near(p, step))

    def b_copy(self, ch, p, d, arriving=False):
        step = 1 - 2 * d
        pos = self.at[1 + p] - 2 if arriving else self.at[1 + p] - step
        ref = self.full.at[ch, :, self.rows(p, pos), pl.ds(d * (D // 2), D // 2)]
        return remote(ref, ref, self.bs.at[ch, p, d], self.br.at[ch, p, d], self.near(p, step))

    def c_copy(self, ch, arriving=False):
        x, y, z, c = self.at
        half = 1 - c if arriving else c
        ref = self.full.at[ch, :, pl.ds(pl.multiple_of(half * HALF, 8), HALF)]
        return remote(ref, ref, self.cs.at[ch], self.cr.at[ch], device(x, y, z, 1 - c))

    def send(self, ch):
        for p in (0, 1):
            for rel in (1, 3, 2):
                self.x_copy(ch, p, rel).start()

    def from_x(self, k):
        for p in (0, 1):
            for rel in (1, 2, 3):
                self.x_copy(k, p, rel).wait_recv()
        for p, d in self.BOTH:
            self.a_copy(k, p, d).start()

    def onward(self, k):
        for p, d in self.BOTH:
            self.a_copy(k, p, d, True).wait_recv()
        for p, d in self.BOTH:
            self.b_copy(k, p, d).start()

    def to_core(self, k):
        for p, d in self.BOTH:
            self.b_copy(k, p, d, True).wait_recv()
        self.c_copy(k).start()

    def go(self, *steps):
        for step in steps:
            (self.from_x, self.onward, self.to_core)["xoc".index(step[0])](int(step[1:]))

    def arrive(self, ch):
        self.c_copy(ch, True).wait_recv()

    def end(self):
        def sent(ch):
            for p in (0, 1):
                for rel in (1, 2, 3):
                    self.x_copy(ch, p, rel).wait_send()
            for p, d in self.BOTH:
                self.a_copy(ch, p, d).wait_send()
                self.b_copy(ch, p, d).wait_send()
            self.c_copy(ch).wait_send()

        loop(CHUNKS, sent)


class Nowhere:
    end = lambda self: None
    send = arrive = lambda self, k: None
    go = lambda self, *steps: None


PAIR_AT = (0, 256, 384, 512)
THIRD_AT = (128, 192, 640, 704)


def repack_heads(st, wb):
    for a in range(2):
        for r in range(4):
            to, third = a * 768 + PAIR_AT[r], a * 768 + THIRD_AT[r]
            wb[to : to + 128] = st[r, a * 192 : a * 192 + 128].astype(bf)
            wb[third : third + 64] = st[r, a * 192 + 128 : a * 192 + 192].astype(bf)


def repack_hidden(st, wb):
    for a in range(3):
        for r in range(4):
            to = a * 512 + r * 128
            wb[to : to + 128] = st[r, a * 128 : a * 128 + 128].astype(bf)


def transpose_to(dst, src):
    for t in range(NB):
        dst[:, t * T : (t + 1) * T] = src[t * T : (t + 1) * T, :].T


def rms(r):
    return lax.rsqrt(jnp.mean(r * r, axis=-1, keepdims=True) + EPS)


def rope(v, cs, sl, sr):
    return v * cs + pltpu.roll(v, 96, 1) * sl + pltpu.roll(v, 32, 1) * sr


def rope_sides(sn):
    first = (lane(sn.shape) % 64) < 32
    return jnp.where(first, -sn, 0.0), jnp.where(first, 0.0, sn)


def head_lanes(h, shape):
    at = lane(shape)
    mine = at < 64 if h == 0 else at >= 64
    base = 64 if h == 0 else 0
    return mine, at - base


def project_scores(u, w, cs, sn, length, qa, ka, k):
    def step(t):
        at = block(t)
        ut = u[at]
        c = cs[at]
        sl, sr = rope_sides(sn[at])
        shape = (T, 128)
        bias = jnp.where(line(shape) + t * T < length, 0.0, NEG)
        val = nt(ut, w[0:768])
        for p in range(6):
            q_p = rope(val[:, p * 128 : p * 128 + 128], c, sl, sr)
            for h in range(2):
                mine, side = head_lanes(h, shape)
                qa[2 * p + h, at] = jnp.where(mine, q_p, jnp.where(side == 0, 1.0, 0.0)).astype(bf)
        val = nt(ut, w[768:1536])
        for p in range(6):
            k_p = rope(val[:, p * 128 : p * 128 + 128], c, sl, sr)
            k[p, at] = k_p.astype(bf)
            for h in range(2):
                mine, side = head_lanes(h, shape)
                other = jnp.where(side == 0, bias, jnp.where(side < 4, -1.0, 0.0))
                ka[2 * p + h, at] = jnp.where(mine, k_p, other).astype(bf)

    loop(NB, step)


def project_values(u, w, va, v):
    def step(t):
        at = block(t)
        val = nt(u[at], w[0:768])
        for p in range(6):
            v_p = val[:, p * 128 : p * 128 + 128]
            v[p, at] = v_p.astype(bf)
            for h in range(2):
                mine, side = head_lanes(h, (T, 128))
                va[2 * p + h, at] = jnp.where(mine, v_p, jnp.where((side >= 1) & (side < 4), -1.0, 0.0)).astype(bf)

    loop(NB, step)


def attend(qa, ka, vt, o, ob, lse, tick):
    def pair(p):
        at_l = pl.ds(pl.multiple_of(p * 128, 128), 128)
        for i in range(NB):
            n = (i + 1) * T
            rows = pl.ds(i * T, T)
            diag = line((T, T)) <= lane((T, T))
            outs, outl = [], []
            for h in range(2):
                s = nt(ka[2 * p + h, 0:n], qa[2 * p + h, rows])
                tail = jnp.where(diag, s[n - T :], NEG)
                s = tail if i == 0 else jnp.concatenate([s[: n - T], tail], axis=0)
                m = jnp.max(s, axis=0, keepdims=True) * SCALE2
                e = jnp.exp2(s * SCALE2 - m)
                tot = jnp.sum(e, axis=0, keepdims=True)
                pr = e * (1.0 / tot)
                pb = pr.astype(bf)
                main = nn(vt[p, h * 64 : h * 64 + 64, 0:n], pb)
                rest = (pr - pb.astype(f32)).astype(bf)
                outs.append(main)
                outl.append(main + nn(vt[p, h * 64 : h * 64 + 64, 0:n], rest))
                lse[pl.ds(p * 2 + h, 1), rows] = m + jnp.log2(tot)
            ob[rows, at_l] = jnp.concatenate(outs, axis=0).T.astype(bf)
            o[rows, at_l] = jnp.concatenate(outl, axis=0).T
        tick(p)

    loop(6, pair)


def three(v):
    hi = v.astype(bf).astype(f32)
    mid = (v - hi).astype(bf).astype(f32)
    low = (v - hi - mid).astype(bf).astype(f32)
    return (hi + pltpu.roll(mid, 16, 1) + pltpu.roll(low, 32, 1)).astype(bf)


def spread_table():
    table = np.zeros((128, 12 * 128), np.float32)
    for h in range(12):
        for j in range(3):
            table[16 * j + h, h * 128 + (65 if h % 2 == 0 else 1) + j] = 1.0
    return table.astype(ml_dtypes.bfloat16)


FWD_OUT = [
    ((CHUNKS, 1536, D), bf),
    ((2, 2, D, S), bf),
    ((2, 12, S, 128), bf),
    ((2, 12, S, 128), bf),
    ((2, 12, S, 128), bf),
    ((2, 6, 128, S), bf),
    ((2, S, D), f32),
    ((2, S, 256), bf),
    ((2, 4, S, 512), bf),
    ((2, 4, S, 512), bf),
    ((2, 4, S, 128), bf),
    ((4, S, D), f32),
    ((S, D), f32),
]
FWD_VMEM = [
    ((S, D), f32),
    ((2, 4, ROWS, D), f32),
    ((2, 1536, D), bf),
    ((12, S, 128), bf),
    ((12, S, 128), bf),
    ((12, S, 128), bf),
    ((6, S, 128), bf),
    ((6, S, 128), bf),
    ((6, 128, S), bf),
    ((6, 128, S), bf),
    ((S, D), f32),
    ((S, D), bf),
    ((128, S), f32),
    ((S, D), bf),
    ((2, D, S), bf),
    ((S, D), f32),
    ((S, D), f32),
    ((2, 2, 512, 512), bf),
    ((4, S, 128), bf),
    ((3, 192, D), bf),
    ((192, D), bf),
    ((2, D, 512), bf),
    ((512, D), bf),
]


def fwd_kernel(comm, length_ref, wq, wk, wv, wo, wg, wu, wd, x_hbm, cs, sn, gains, spread, *rest):
    own, full, rest = (rest[1], rest[0], rest[2:]) if not comm else (rest[0], rest[1], rest[2:])
    outs, rest = rest[: len(FWD_OUT)], rest[len(FWD_OUT) :]
    w_o, ut_o, qa_o, ka_o, va_o, kt_o, o_o, ob_o, a_o, b_o, hb_o, res_o, out_o = outs
    (x, st, wb, qa, ka, va, k, v, kt, vt, o, ob, lse, u, ut, acc, res, ab, hb, raw_h, raw_o, raw_f, raw_d), rest = (
        rest[: len(FWD_VMEM)],
        rest[len(FWD_VMEM) :],
    )
    load_sem, w_sem, save_sem, ab_sem, own_sem, put_sem = rest[:6]
    net = Gather(own, full, rest[6:]) if comm else Nowhere()
    length = length_ref[0]

    def raw(layer, i):
        src = (wq, wk, wv, wo, wg, wu, wd)[i]
        dst = (raw_h.at[0], raw_h.at[1], raw_h.at[2], raw_o, raw_f.at[0], raw_f.at[1], raw_d)[i]
        return pltpu.make_async_copy(src.at[layer], dst, own_sem.at[i])

    def own_chunks(layer):
        if layer == 0:
            return [st.at[i // 4, i % 4] for i in range(6)]
        return [st.at[1, 2], st.at[1, 3]] + [b.at[pl.ds(i * ROWS, ROWS)] for b in (acc, res) for i in range(2)]

    def put_own(layer, i):
        return pltpu.make_async_copy(own_chunks(layer)[i], own.at[layer * 6 + i], put_sem.at[i])

    def turn(dst, row, src):
        for t in range(3):
            dst[row : row + src.shape[1], t * T : (t + 1) * T] = src[t * T : (t + 1) * T, :].astype(f32).T

    def start_raw(layer):
        for i in range(7):
            raw(layer, i).start()

    def prepare_heads(layer):
        to = own_chunks(layer)
        for n in range(2):
            raw(layer, 2 * n).wait()
            raw(layer, 2 * n + 1).wait()
            to[n][0:192] = raw_h[2 * n].astype(f32)
            to[n][192:384] = (raw_o if n else raw_h.at[1])[...].astype(f32)
            put_own(layer, n).start()

    def prepare_hidden(layer):
        to = own_chunks(layer)
        for i in (4, 5, 6):
            raw(layer, i).wait()
        for f in range(4):
            for i in range(2):
                turn(to[2 + f], i * 128, raw_f.at[i, :, pl.ds(f * 128, 128)])
            to[2 + f][256:384] = raw_d[f * 128 : f * 128 + 128].astype(f32)
            put_own(layer, 2 + f).start()

    def send_own(layer, chunks):
        for i in chunks:
            put_own(layer, i).wait()
            net.send(layer * 6 + i)

    if comm:
        greet()
    start_raw(0)
    x_in = pltpu.make_async_copy(x_hbm, x, save_sem.at[0])
    x_in.start()
    prepare_heads(0)
    if comm:
        greeted()
    send_own(0, (0, 1))
    prepare_hidden(0)
    start_raw(1)
    send_own(0, (2, 3, 4, 5))
    prepare_heads(1)
    prepare_hidden(1)
    send_own(1, range(6))
    x_in.wait()

    def loads(ch, slot):
        return (
            pltpu.make_async_copy(own.at[ch], st.at[slot, 0], load_sem.at[slot, 0]),
            pltpu.make_async_copy(full.at[ch], st.at[slot, pl.ds(1, 3)], load_sem.at[slot, 1]),
        )

    def start_load(ch, slot):
        net.arrive(ch)
        for copy in loads(ch, slot):
            copy.start()

    def put_weights(ch, slot):
        return pltpu.make_async_copy(wb.at[slot], w_o.at[ch], w_sem.at[slot])

    def unpack(ch, slot, repack, first=False):
        for copy in loads(ch, slot):
            copy.wait()
        if not first:
            put_weights(ch, slot).wait()
        repack(st.at[slot], wb.at[slot])
        put_weights(ch, slot).start()

    flying = {}

    def save(name, src, dst, i):
        flying[name] = pltpu.make_async_copy(src, dst, save_sem.at[i])
        flying[name].start()

    def settle(*names):
        for name in names:
            if name in flying:
                flying.pop(name).wait()

    lse[...] = jnp.zeros((128, S), f32)
    for layer in range(2):
        base = layer * 6
        settle("uta")

        def enter(t):
            at = block(t)
            val = x[at]
            if layer:
                val = val * rms(val) * gains[2:3]
            u[at] = val.astype(bf)

        loop(NB, enter)
        transpose_to(ut.at[0], u)
        save("uta", ut.at[0], ut_o.at[layer, 0], 0)
        if layer == 0:
            net.go("x0", "x1", "o0", "o1", "x2", "c0", "c1")
            start_load(0, 0)
        unpack(base, 0, repack_heads, layer == 0)
        settle("qa", "ka", "va", "kt", "o", "ob")
        project_scores(u, wb.at[0], cs, sn, length, qa, ka, k)
        if layer == 0:
            start_load(1, 1)
        unpack(base + 1, 1, repack_heads, layer == 0)
        project_values(u, wb.at[1], va, v)
        for p in range(6):
            transpose_to(kt.at[p], k.at[p])
            transpose_to(vt.at[p], v.at[p])
        save("ka", ka, ka_o.at[layer], 1)
        save("va", va, va_o.at[layer], 2)
        save("kt", kt, kt_o.at[layer], 3)
        net.go(*(("x10", "o8") if layer else ("x3", "o2")))

        def tick(p):
            plans = (
                {1: ("x4", "o3"), 3: ("x5", "c2", "o4"), 5: ("x6", "c3", "o5")},
                {1: ("x11", "o9"), 3: ("o10", "c8"), 5: ("o11", "c9")},
            )
            for at, plan in plans[layer].items():

                @pl.when(p == at)
                def _():
                    net.go(*plan)

        attend(qa, ka, vt, o, ob, lse, tick)
        start_load(base + 2, 0)
        save("o", o, o_o.at[layer], 4)
        save("ob", ob.at[:, pl.ds(0, 256)], ob_o.at[layer], 5)

        def add_lse(t):
            at = block(t)
            val = nn(three(lse[:, at].T * (1.0 / SCALE2)), spread[...])
            for h in range(12):
                qa[h, at] = (qa[h, at].astype(f32) + val[:, h * 128 : h * 128 + 128]).astype(bf)

        loop(NB, add_lse)
        save("qa", qa, qa_o.at[layer], 6)
        settle("res")

        def after(t):
            at = block(t)
            r = x[at] + nn(ob[at], wb[1, 768:1536])
            res[at] = r
            n = r * rms(r)
            if layer == 0:
                h = n * gains[0:1]
                acc[at] = h
                u[at] = h.astype(bf)
            else:
                acc[at] = r
                u[at] = (n * gains[3:4]).astype(bf)

        loop(NB, after)
        save("res", res, res_o.at[2 * layer if layer == 0 else 3], 7)
        settle("utf")
        transpose_to(ut.at[1], u)
        save("utf", ut.at[1], ut_o.at[layer, 1], 8)
        settle("hb")
        net.go(*(("c10", "c11") if layer else ("x7", "c4", "o6")))

        def chunk(f):
            ch = base + 2 + f
            slot = lax.rem(f, 2)

            if layer == 0:
                for at, plan in {1: ("o7", "c5"), 2: ("x8", "c6"), 3: ("c7",)}.items():

                    @pl.when(f == at)
                    def _():
                        net.go(*plan)

            @pl.when(ch + 1 < CHUNKS)
            def _():
                start_load(ch + 1, 1 - slot)

            unpack(ch, slot, repack_hidden)
            w = wb.at[slot]

            def step(t):
                at = block(t, 512)

                def put(j):
                    return pltpu.make_async_copy(ab.at[t, j], (a_o, b_o)[j].at[layer, f, at], ab_sem.at[t, j])

                @pl.when(f >= 1)
                def _():
                    put(0).wait()
                    put(1).wait()

                ub = u[at]
                gate = nt(ub, w[0:512])
                up = nt(ub, w[512:1024])
                sig = 1.0 / (1.0 + jnp.exp(-gate))
                a = gate * sig
                hid = (a * up).astype(bf)
                ab[t, 0] = a.astype(bf)
                ab[t, 1] = (up * (sig + a * (1.0 - sig))).astype(bf)
                hb[f, at] = hid[:, 0:128]
                acc[at] = acc[at] + nn(hid, w[1024:1536])
                put(0).start()
                put(1).start()

            loop(2, step)

        loop(4, chunk)
        for t in range(2):
            for j in range(2):
                pltpu.make_async_copy(ab.at[t, j], a_o.at[layer, 0, block(0, 512)], ab_sem.at[t, j]).wait()
        save("hb", hb, hb_o.at[layer], 9)
        if layer == 0:
            net.go("x9")
            start_load(7, 1)
            settle("res")

            def leave(t):
                at = block(t)
                r = acc[at]
                res[at] = r
                x[at] = r * rms(r) * gains[1:2]

            loop(NB, leave)
            save("res", res, res_o.at[1], 7)
            save("y", x, res_o.at[2], 10)
        else:
            settle("y")

            def last(t):
                at = block(t)
                x[at] = jnp.where(line((T, 1)) + t * T < length, acc[at], 0.0)

            loop(NB, last)
            save("out", x, out_o, 11)
    settle(*list(flying))
    for slot in range(2):
        put_weights(0, slot).wait()
    net.end()


def whole(memory):
    return pl.BlockSpec(memory_space=memory)


def forward(length, weights, x, cs, sn, gains, spread, full=None):
    comm = full is None
    hbm, vmem = whole(pl.ANY), whole(pltpu.VMEM)
    extra = [((CHUNKS, ROWS, D), f32)] + ([((CHUNKS, 3, ROWS, D), f32)] if comm else [])
    outs = [jax.ShapeDtypeStruct(s, d) for s, d in extra + FWD_OUT]
    dma = pltpu.SemaphoreType.DMA
    result = pl.pallas_call(
        lambda *refs: fwd_kernel(comm, *refs),
        out_shape=outs,
        in_specs=[whole(pltpu.SMEM)] + [hbm] * 8 + [vmem] * 4 + ([] if comm else [hbm]),
        out_specs=[hbm] * len(outs),
        scratch_shapes=[pltpu.VMEM(s, d) for s, d in FWD_VMEM]
        + [dma((2, 2)), dma((2,)), dma((12,)), dma((2, 2)), dma((7,)), dma((6,))]
        + ([dma(s) for s in Gather.SEMS] if comm else []),
        compiler_params=pltpu.CompilerParams(
            vmem_limit_bytes=63 * 2**20,
            **(dict(collective_id=0, has_side_effects=True) if comm else {}),
        ),
    )(length, *weights, x, cs, sn, gains, spread, *([] if comm else [full]))
    return result[len(extra) :]


GROUPS = 6
GRAD_ROWS = 24


class Scatter:
    SEMS = [(GROUPS,)] * 2 + [(GROUPS, 2, 3)] * 4 + [(7,)] * 2
    VMEM = [
        ((2, 2, 16, GRAD_ROWS, D), f32),
        ((4, 16, GRAD_ROWS, D), f32),
        ((2, 2, 3, 4, GRAD_ROWS, D // 2), f32),
        ((2, 2, 3, GRAD_ROWS, D // 2), f32),
        ((8, D), f32),
        ((7, 8, D), f32),
    ]

    def __init__(self, out, bufs, sems):
        self.out = out
        self.grads, self.sums, self.one, self.two, self.gain, self.gains_in = bufs
        self.cs, self.cr, self.s1, self.r1, self.s2, self.r2, self.gs, self.gr = sems
        self.at = place()

    def peer(self, along, k):
        x, y, z, c = self.at
        return device(x, y + k, z, c) if along == 0 else device(x, y, z + k, c)

    def greet(self):
        x, y, z, c = self.at
        bar = pltpu.get_barrier_semaphore()
        to = [self.peer(a, k) for a in (0, 1) for k in (1, 2, 3)] + [device(x, y, z, 1 - c)]
        for other in to:
            pl.semaphore_signal(bar, inc=1, device_id=other, device_id_type=MESH)

    def greeted(self):
        pl.semaphore_wait(pltpu.get_barrier_semaphore(), 7)

    def columns(self, part):
        return pl.ds(part * (D // 2), D // 2)

    def core_copy(self, g):
        x, y, z, c = self.at
        return remote(
            self.grads.at[lax.rem(g, 2), 1 - c],
            self.sums.at[lax.rem(g, 4)],
            self.cs.at[g],
            self.cr.at[g],
            device(x, y, z, 1 - c),
        )

    def four(self, g, part, pos):
        ref = self.sums.at[lax.rem(g, 4)]
        if part == 0:
            return ref.at[pl.ds(pos * 4, 4), :, self.columns(0)]
        return ref

    def one_copies(self, g, part, k):
        pos = lax.rem(self.at[1 + part] + k, 4)
        slot = lax.rem(g, 2)
        dst = self.one.at[slot, part, 3 - k]
        send, recv, to = self.s1.at[g, part, k - 1], self.r1.at[g, part, 3 - k], self.peer(part, k)
        sums = self.sums.at[lax.rem(g, 4)]
        if part == 0:
            return [remote(sums.at[pl.ds(pos * 4, 4), :, self.columns(0)], dst, send, recv, to)]
        return [remote(sums.at[i * 4 + pos, :, self.columns(1)], dst.at[i], send, recv, to) for i in range(4)]

    def one_wait(self, g, part, k):
        dst = self.one.at[lax.rem(g, 2), part, k - 1]
        return remote(dst, dst, self.s1.at[g, part, k - 1], self.r1.at[g, part, k - 1], self.peer(part, k))

    def two_copy(self, g, part, k):
        along = 1 - part
        pos = lax.rem(self.at[1 + along] + k, 4)
        _, y, z, _ = self.at
        index = y * 4 + pos if part == 0 else pos * 4 + z
        return remote(
            self.sums.at[lax.rem(g, 4), index, :, self.columns(part)],
            self.two.at[lax.rem(g, 2), part, 3 - k],
            self.s2.at[g, part, k - 1],
            self.r2.at[g, part, 3 - k],
            self.peer(along, k),
        )

    def two_wait(self, g, part, k):
        dst = self.two.at[lax.rem(g, 2), part, k - 1]
        return remote(dst, dst, self.s2.at[g, part, k - 1], self.r2.at[g, part, k - 1], self.peer(1 - part, k))

    def gain_copy(self, step, k=0):
        x, y, z, c = self.at
        if step == 0:
            i = j = 0
            to = device(x, y, z, 1 - c)
        else:
            i, j = 3 * step - 3 + k, 3 * step - 3 + 4 - k
            to = self.peer(step - 1, k)
        return remote(self.gain, self.gains_in.at[j], self.gs.at[i], self.gr.at[j], to)

    def stage0(self, g):
        self.core_copy(g).start()

    def stage1(self, g):
        copy = self.core_copy(g)
        copy.wait_recv()
        c = self.at[3]
        slot, ring = lax.rem(g, 2), lax.rem(g, 4)

        def add(i):
            self.sums[ring, i] = self.sums[ring, i] + self.grads[slot, c, i]

        loop(16, add)
        for part in (0, 1):
            for k in (1, 3, 2):
                for one in self.one_copies(g, part, k):
                    one.start()
        copy.wait_send()

    def stage2(self, g):
        for part in (0, 1):
            for k in (1, 2, 3):
                self.one_wait(g, part, k).wait_recv()
        _, y, z, _ = self.at
        slot, ring = lax.rem(g, 2), lax.rem(g, 4)

        def add(i):
            for part in (0, 1):
                at = (y * 4 + i) if part == 0 else (i * 4 + z)
                cols = pl.ds(part * (D // 2), D // 2)
                got = self.one[slot, part, 0, i] + self.one[slot, part, 1, i] + self.one[slot, part, 2, i]
                self.sums[ring, at, :, cols] = self.sums[ring, at, :, cols] + got

        for part in (0, 1):
            for k in (1, 2, 3):
                self.one_sent(g, part, k)
        loop(4, add)
        for part in (0, 1):
            for k in (1, 3, 2):
                self.two_copy(g, part, k).start()

    def one_sent(self, g, part, k):
        for one in self.one_copies(g, part, k):
            one.wait_send()

    def stage3(self, g):
        for part in (0, 1):
            for k in (1, 2, 3):
                self.two_wait(g, part, k).wait_recv()
        _, y, z, _ = self.at
        slot, ring = lax.rem(g, 2), lax.rem(g, 4)
        for part in (0, 1):
            cols = pl.ds(part * (D // 2), D // 2)
            got = self.two[slot, part, 0] + self.two[slot, part, 1] + self.two[slot, part, 2]
            self.out[g, :, cols] = self.sums[ring, y * 4 + z, :, cols] + got
        for part in (0, 1):
            for k in (1, 2, 3):
                self.two_copy(g, part, k).wait_send()

    def tick(self, n):
        @pl.when((n >= 3) & (n < GROUPS + 3))
        def _():
            self.stage3(n - 3)

        @pl.when((n >= 2) & (n < GROUPS + 2))
        def _():
            self.stage2(n - 2)

        @pl.when((n >= 1) & (n < GROUPS + 1))
        def _():
            self.stage1(n - 1)

        @pl.when(n < GROUPS)
        def _():
            self.stage0(n)

    def gain_start(self, step):
        if step == 0:
            self.gain_copy(0).start()
        else:
            for k in (1, 2, 3):
                self.gain_copy(step, k).start()

    def gain_finish(self, step):
        copies = [self.gain_copy(0)] if step == 0 else [self.gain_copy(step, k) for k in (1, 2, 3)]
        for copy in copies:
            copy.wait()
        first = 0 if step == 0 else 3 * step - 2
        for j in range(first, first + len(copies)):
            self.gain[...] = self.gain[...] + self.gains_in[j]


class Keep:
    VMEM = Scatter.VMEM

    def __init__(self, out, bufs, sems):
        self.out, self.grads, self.gain, self.sem = out, bufs[0], bufs[4], sems[0]

    def greet(self):
        pass

    greeted = greet

    def tick(self, n):
        @pl.when(n < GROUPS)
        def _():
            copy = pltpu.make_async_copy(self.grads.at[lax.rem(n, 2)], self.out.at[n], self.sem)
            copy.start()
            copy.wait()

    def gain_start(self, step):
        pass

    gain_finish = gain_start


BWD_VMEM = [
    ((S, D), f32),
    ((S, D), f32),
    ((S, D), f32),
    ((S, D), f32),
    ((S, D), bf),
    ((D, S), bf),
    ((D, S), bf),
    ((2, 1536, D), bf),
    ((2, 2, 512, 512), bf),
    ((12, S, 128), bf),
    ((12, S, 128), bf),
    ((12, S, 128), bf),
    ((12, S, 128), bf),
    ((6, 128, S), bf),
    ((S, D), bf),
    ((S, D), bf),
    ((S, D), bf),
    ((128, S), f32),
    ((4, S, 256), bf),
]


def bwd_kernel(comm, length_ref, cot, w, uts, qas, kas, vas, kts, os_, obs, as_, bs, hbs, ress, cs, sn, gains, spread, *rest):
    input_grad, gain_out, grad_out = rest[:3]
    rest = rest[3:]
    (e, acc, res, mix, eb, ebt, ut, wb, ab, qa, ka, va, da, kt, dq, dk, dv, dqt, own), rest = (
        rest[: len(BWD_VMEM)],
        rest[len(BWD_VMEM) :],
    )
    bufs, rest = rest[: len(Scatter.VMEM)], rest[len(Scatter.VMEM) :]
    load_sem, w_sem, ab_sem, rest = rest[0], rest[1], rest[2], rest[3:]
    net = (Scatter if comm else Keep)(grad_out, bufs, rest)
    grads, gain = bufs[0], bufs[4]
    length = length_ref[0]

    flying = {}

    def fetch(name, src, dst, i):
        flying[name] = pltpu.make_async_copy(src, dst, load_sem.at[i])
        flying[name].start()

    def need(*names):
        for name in names:
            flying.pop(name).wait()

    def weights(ch, slot):
        return pltpu.make_async_copy(w.at[ch], wb.at[slot], w_sem.at[slot])

    def factors(layer, f, t):
        return [
            pltpu.make_async_copy(src.at[layer, f, block(t, 512)], ab.at[t, j], ab_sem.at[t, j])
            for j, src in ((0, as_), (1, bs))
        ]

    def round_grad():
        def step(t):
            at = block(t)
            eb[at] = e[at].astype(bf)

        loop(NB, step)
        transpose_to(ebt, eb)

    def norm_back(incoming, r, row):
        fac = rms(r)
        n = r * fac
        gain[row : row + 1] = gain[row : row + 1] + jnp.sum(incoming * n, axis=0, keepdims=True)
        inner = incoming * gains[row : row + 1]
        return fac * (inner - n * jnp.mean(inner * n, axis=-1, keepdims=True))

    def place_rows(slot, i, cols, val):
        for b in range(8):
            grads[slot, b % 2, i * 4 + b // 2, :, cols] = val[b * 24 : b * 24 + 24]

    def heads_in(layer):
        fetch("qa", qas.at[layer], qa, 3)
        fetch("ka", kas.at[layer], ka, 4)
        fetch("va", vas.at[layer], va, 5)
        fetch("kt", kts.at[layer], kt, 6)
        fetch("mix", os_.at[layer], mix, 9)

    net.greet()
    gain[...] = jnp.zeros((8, D), f32)
    fetch("cot", cot, e, 0)
    fetch("ut", uts.at[1, 1], ut, 1)
    fetch("res", ress.at[3], res, 2)
    weights(8, 0).start()
    for t in range(2):
        for copy in factors(1, 0, t):
            copy.start()
    heads_in(1)
    need("cot")

    def mask(t):
        at = block(t)
        e[at] = jnp.where(line((T, 1)) + t * T < length, e[at], 0.0)

    loop(NB, mask)

    for layer in (1, 0):
        base = layer * 6
        group = 3 * (1 - layer)
        round_grad()

        def clear(t):
            acc[block(t)] = jnp.zeros((T, D), f32)

        loop(NB, clear)
        need("ut")
        if layer:
            net.greeted()

        def half(hh):
            for i in range(2):
                pltpu.make_async_copy(
                    hbs.at[layer, 2 * hh + i], own.at[2, :, pl.ds(i * 128, 128)], load_sem.at[10 + i]
                ).start()

            for i in range(2):
                f = 2 * hh + i
                ch = base + 2 + f
                weights(ch, i).wait()
                if i == 0:
                    weights(ch + 1, 1).start()
                else:

                    @pl.when(hh == 0)
                    def _():
                        weights(ch + 1, 0).start()

                    @pl.when(hh == 1)
                    def _():
                        weights(base, 0).start()

                def step(t):
                    at = block(t, 512)
                    for copy in factors(layer, f, t):
                        copy.wait()
                    a, b = ab[t, 0].astype(f32), ab[t, 1].astype(f32)
                    dh = nt(eb[at], wb[i, 1024:1536])
                    dg = (dh * b).astype(bf)
                    du = (dh * a).astype(bf)
                    own[0, at, i * 128 : i * 128 + 128] = dg[:, 0:128]
                    own[1, at, i * 128 : i * 128 + 128] = du[:, 0:128]
                    acc[at] = acc[at] + nn(dg, wb[i, 0:512]) + nn(du, wb[i, 512:1024])

                    @pl.when(f < 3)
                    def _():
                        for copy in factors(layer, f + 1, t):
                            copy.start()

                loop(2, step)
            for i in range(2):
                pltpu.make_async_copy(
                    hbs.at[layer, 2 * hh + i], own.at[2, :, pl.ds(i * 128, 128)], load_sem.at[10 + i]
                ).wait()
            slot = lax.rem(group + hh, 2)

            def outer(i):
                at = block(i, 192)
                vals = nn(ut[at], own[0]), nn(ut[at], own[1]), nn(ebt[at], own[2])
                for n in range(3):
                    place_rows(slot, i, pl.ds(n * 256, 256), vals[n])

            loop(4, outer)
            net.tick(group + hh)

        loop(2, half)
        weights(base + 1, 1).start()
        fetch("ut", uts.at[layer, 0], ut, 1)
        fetch("ob", obs.at[layer], own.at[3], 7)
        need("res")

        def through(t):
            at = block(t)
            if layer:
                e[at] = e[at] + norm_back(acc[at], res[at], 3)
            else:
                e[at] = norm_back(e[at] + acc[at], res[at], 0)

        loop(NB, through)
        if layer:
            fetch("res", ress.at[2], res, 2)
        round_grad()
        if layer == 0:
            net.gain_start(0)
        weights(base, 0).wait()
        weights(base + 1, 1).wait()
        need("mix")
        owner = jnp.where(line((D, 128)) // 64 == lane((D, 128)), 1.0, 0.0).astype(bf)

        def mixed_back(t):
            at = block(t)
            val = nt(eb[at], wb[1, 768:1536]).astype(bf)
            prod = val.astype(f32) * mix[at]
            hi = prod.astype(bf)
            low = (prod - hi.astype(f32)).astype(bf)
            inner = nn(three(nn(hi, owner) + nn(low, owner)), spread[...])
            for h in range(12):
                mine, _ = head_lanes(h % 2, (T, 128))
                pair = val[:, (h // 2) * 128 : (h // 2) * 128 + 128]
                da[h, at] = jnp.where(mine, pair, inner[:, h * 128 : h * 128 + 128].astype(bf))

        loop(NB, mixed_back)
        if layer:
            fetch("below", ress.at[1], mix, 9)
        need("qa", "ka", "va", "kt", "ut", "ob")
        low = lane((T, 128)) < 64

        def pair(p):
            at_l = pl.ds(pl.multiple_of(p * 128, 128), 128)
            for j in range(NB):
                ks, qs = pl.ds(j * T, T), pl.ds(j * T, S - j * T)
                diag = line((T, T)) <= lane((T, T))
                dvs, dks = [], []
                for h in range(2):
                    hd = 2 * p + h
                    s = nt(ka[hd, ks], qa[hd, qs])
                    dp = nt(va[hd, ks], da[hd, qs])
                    pr = jnp.exp2(s * SCALE2)
                    head = jnp.where(diag, pr[:, :T], 0.0)
                    pr = head if j == NB - 1 else jnp.concatenate([head, pr[:, T:]], axis=1)
                    ds = (pr * dp).astype(bf)
                    dvs.append(nn(pr.astype(bf), da[hd, qs]))
                    dks.append(nn(ds, qa[hd, qs]))
                    val = nn(kt[p, h * 64 : h * 64 + 64, ks], ds)
                    if j == 0:
                        dqt[h * 64 : h * 64 + 64, :] = val
                    else:
                        dqt[h * 64 : h * 64 + 64, j * T :] = dqt[h * 64 : h * 64 + 64, j * T :] + val
                dv[ks, at_l] = jnp.where(low, dvs[0], dvs[1]).astype(bf)
                sl, sr = rope_sides(sn[ks])
                dk_j = jnp.where(low, dks[0], dks[1]) * 0.125
                dk[ks, at_l] = rope(dk_j, cs[ks], -sl, -sr).astype(bf)
            for j in range(NB):
                ks = pl.ds(j * T, T)
                sl, sr = rope_sides(sn[ks])
                dq_j = dqt[:, j * T : j * T + T].T * 0.125
                dq[ks, at_l] = rope(dq_j, cs[ks], -sl, -sr).astype(bf)

        loop(2, pair)
        slot = (group + 2) % 2

        def own_heads(i):
            at = block(i, 192)
            vals = [nn(ut[at], dq[:, 0:256]), nn(ut[at], dk[:, 0:256]), nn(ut[at], dv[:, 0:256]), nn(ebt[at], own[3])]
            left = lane((192, 128)) < 64
            tiles = [v[:, 0:128] for v in vals] + [
                jnp.where(left, vals[n][:, 128:256], pltpu.roll(vals[n + 1][:, 128:256], 64, 1)) for n in (0, 2)
            ]
            for n, tile in enumerate(tiles):
                place_rows(slot, i, pl.ds(n * 128, 128), tile)

        loop(4, own_heads)
        net.tick(group + 2)
        if layer:
            fetch("ut", uts.at[0, 1], ut, 1)
            loop(4, lambda p: pair(p + 2))
        else:
            net.gain_finish(0)
            net.gain_start(1)
            loop(2, lambda p: pair(p + 2))
            net.tick(6)
            net.gain_finish(1)
            net.gain_start(2)
            loop(2, lambda p: pair(p + 4))
            net.tick(7)
            net.gain_finish(2)

        def into(t):
            at = block(t)
            val = nn(dq[at], wb[0, 0:768]) + nn(dk[at], wb[0, 768:1536]) + nn(dv[at], wb[1, 0:768])
            acc[at] = val

        loop(NB, into)
        if layer:
            weights(2, 0).start()
            for t in range(2):
                for copy in factors(0, 0, t):
                    copy.start()
            need("res", "below")

            def between(t):
                at = block(t)
                e[at] = norm_back(e[at] + norm_back(acc[at], res[at], 2), mix[at], 1)

            loop(NB, between)
            fetch("res", ress.at[0], res, 2)
            heads_in(0)
        else:

            def last(t):
                at = block(t)
                acc[at] = e[at] + acc[at]

            loop(NB, last)
            done = pltpu.make_async_copy(acc, input_grad, load_sem.at[0])
            done.start()
            gain_out[...] = gain[...]
            net.tick(8)
            done.wait()


def backward(comm, length, cot, kept, cs, sn, gains, spread):
    hbm, vmem = whole(pl.ANY), whole(pltpu.VMEM)
    dma = pltpu.SemaphoreType.DMA
    w, uts, qas, kas, vas, kts, os_, obs, as_, bs, hbs, ress = kept[:12]
    grad = (GROUPS, GRAD_ROWS, D) if comm else (GROUPS, 2, 16, GRAD_ROWS, D)
    return pl.pallas_call(
        lambda *refs: bwd_kernel(comm, *refs),
        out_shape=[jax.ShapeDtypeStruct(s, f32) for s in [(S, D), (8, D), grad]],
        in_specs=[whole(pltpu.SMEM)] + [hbm] * 13 + [vmem] * 4,
        out_specs=[hbm, vmem, vmem if comm else hbm],
        scratch_shapes=[pltpu.VMEM(s, d) for s, d in BWD_VMEM + Scatter.VMEM]
        + [dma((12,)), dma((2,)), dma((2, 2))]
        + ([dma(s) for s in Scatter.SEMS] if comm else [dma]),
        compiler_params=pltpu.CompilerParams(
            vmem_limit_bytes=63 * 2**20,
            **(dict(collective_id=1, has_side_effects=True) if comm else {}),
        ),
    )(length, cot, w, uts, qas, kas, vas, kts, os_, obs, as_, bs, hbs, ress, cs, sn, gains, spread)


def finish_kernel(out_in, grad_in, sums, gain, out, grad, q, k, v, o, gate, up, down, gains, last, big, sem):
    parts = [(src, dst, t) for src, dst in ((out_in, out), (grad_in, grad)) for t in range(NB)]

    def get(n):
        src, _, t = parts[n]
        return pltpu.make_async_copy(src.at[pl.ds(t * T, T)], big.at[n], sem.at[n])

    def put(n):
        _, dst, t = parts[n]
        return pltpu.make_async_copy(big.at[n], dst.at[pl.ds(t * T, T)], sem.at[n])

    for n in range(len(parts)):
        get(n).start()
    for layer in range(2):
        heads = sums.at[5 - 3 * layer]
        thirds = [heads[:, 512:640], heads[:, 640:768]]
        thirds = [thirds[0], pltpu.roll(thirds[0], 64, 1), thirds[1], pltpu.roll(thirds[1], 64, 1)]
        for n, to in enumerate((q, k, v, o)):
            to[layer, :, 0:128] = heads[:, n * 128 : n * 128 + 128]
            to[layer, :, 128:192] = thirds[n][:, 0:64]
        for half in range(2):
            for n, to in enumerate((gate, up, down)):
                to[layer, :, half * 256 : half * 256 + 256] = sums[3 - 3 * layer + half, :, n * 256 : n * 256 + 256]
    mine = pltpu.roll(gain[...], lax.rem(D - lax.axis_index("dp") * GRAD_ROWS, D), 1)
    gains[...] = mine[0:3, 0:GRAD_ROWS]
    last[...] = mine[3:4, 0:GRAD_ROWS]
    for n in range(len(parts)):
        get(n).wait()
        put(n).start()
    for n in range(len(parts)):
        put(n).wait()


def finish(out, grad, sums, gain):
    hbm, vmem = whole(pl.ANY), whole(pltpu.VMEM)
    shapes = [(S, D)] * 2 + [(2, GRAD_ROWS, 192)] * 4 + [(2, GRAD_ROWS, 512)] * 3 + [(3, GRAD_ROWS), (1, GRAD_ROWS)]
    return pl.pallas_call(
        finish_kernel,
        out_shape=[jax.ShapeDtypeStruct(s, f32) for s in shapes],
        in_specs=[hbm, hbm, vmem, vmem],
        out_specs=[hbm, hbm] + [vmem] * 9,
        scratch_shapes=[pltpu.VMEM((2 * NB, T, D), f32), pltpu.SemaphoreType.DMA((2 * NB,))],
        compiler_params=pltpu.CompilerParams(vmem_limit_bytes=60 * 2**20),
    )(out, grad, sums, gain)


def rope_tables():
    freq = (10000.0 ** (-np.arange(32) * 2.0 / 64)).astype(np.float32)
    angle = (np.arange(S, dtype=np.float32)[:, None] * freq[None, :]).astype(np.float64)
    return tuple(np.tile(v.astype(np.float32), (1, 4)) for v in (np.cos(angle), np.sin(angle)))


def local(block_input, lengths, cotangent, w_query, w_key, w_value, w_output, w_gate, w_up, w_down, gains):
    cs, sn = rope_tables()
    spread = spread_table()
    heads = [jnp.swapaxes(w, 1, 2) for w in (w_query, w_key, w_value)]
    weights = (*heads, w_output, w_gate, w_up, w_down)
    kept = forward(lengths, weights, block_input, cs, sn, gains, spread)
    input_grad, gain_sums, grads = backward(True, lengths, cotangent, kept, cs, sn, gains, spread)
    out, input_grad, q, k, v, o, gate, up, down, gain_grads, last = finish(kept[12], input_grad, grads, gain_sums)
    return (out, input_grad, q, k, v, jnp.swapaxes(o, 1, 2), gate, up, jnp.swapaxes(down, 1, 2), gain_grads, last[0])


def solution(mesh):
    rows, cols, deep = P("dp", None), P(None, None, "tensor"), P(None, "tensor", None)
    return jax.shard_map(
        local,
        mesh=mesh,
        in_specs=(rows, P("dp"), rows, cols, cols, cols, deep, cols, cols, deep, P()),
        out_specs=(rows, rows)
        + (P(None, "dp", "tensor"),) * 3
        + (P(None, "tensor", "dp"),)
        + (P(None, "dp", "tensor"),) * 2
        + (P(None, "tensor", "dp"), P(None, "dp"), P("dp")),
        check_vma=False,
    )
```

```python
import math

import jax
import jax.numpy as jnp
import ml_dtypes
import numpy as np
from jax import lax
from jax.experimental import pallas as pl
from jax.experimental.pallas import tpu as pltpu
from jax.sharding import PartitionSpec as P

bf, f32 = jnp.bfloat16, jnp.float32
MESH = pl.DeviceIdType.MESH

CHUNKS, ROWS, D, S, T = 12, 384, 768, 1024, 256
NB = S // T
HALF, QUART, PIECE = ROWS // 2, ROWS // 4, ROWS // 16
UNIT = 128 * 4
SCALE2 = 0.125 * math.log2(math.e)
EPS = 1e-5
NEG = -1e30


def nt(a, b):
    return lax.dot_general(a, b, (((1,), (1,)), ((), ())), preferred_element_type=f32)


def nn(a, b):
    return lax.dot_general(a, b, (((1,), (0,)), ((), ())), preferred_element_type=f32)


def lane(shape):
    return lax.broadcasted_iota(jnp.int32, shape, len(shape) - 1)


def line(shape):
    return lax.broadcasted_iota(jnp.int32, shape, len(shape) - 2)


def loop(count, body):
    lax.fori_loop(0, count, lambda i, c: (body(i), c)[1], 0)


def block(t, size=T):
    return pl.ds(pl.multiple_of(t * size, size), size)


def place():
    d = lax.axis_index("dp")
    return lax.axis_index("tensor"), d // 8, (d // 2) % 4, d % 2


def device(x, y, z, c):
    return (((y % 4) * 4 + (z % 4)) * 2 + c, x % 4)


def remote(src, dst, send, recv, to):
    return pltpu.make_async_remote_copy(
        src_ref=src, dst_ref=dst, send_sem=send, recv_sem=recv, device_id=to, device_id_type=MESH
    )


def greet():
    x, y, z, c = place()
    bar = pltpu.get_barrier_semaphore()
    for to in (
        device(x + 1, y, z, c),
        device(x + 2, y, z, c),
        device(x + 3, y, z, c),
        device(x, y + 1, z, c),
        device(x, y + 3, z, c),
        device(x, y, z + 1, c),
        device(x, y, z + 3, c),
        device(x, y, z, 1 - c),
    ):
        pl.semaphore_signal(bar, inc=1, device_id=to, device_id_type=MESH)


def greeted():
    pl.semaphore_wait(pltpu.get_barrier_semaphore(), 8)


class Gather:
    SEMS = [(CHUNKS, 2, 3)] * 2 + [(CHUNKS, 2, 2)] * 4 + [(CHUNKS,)] * 2
    BOTH = [(p, d) for p in (0, 1) for d in (0, 1)]

    def __init__(self, own, full, sems):
        self.own, self.full = own, full
        self.xs, self.xr, self.as_, self.ar, self.bs, self.br, self.cs, self.cr = sems
        self.at = place()

    def rows(self, p, pos):
        c = self.at[3]
        return pl.ds(pl.multiple_of(c * HALF + p * QUART + ((pos + 4) % 4) * PIECE, 8), PIECE)

    def near(self, p, step):
        x, y, z, c = self.at
        return device(x, y + 4 + step, z, c) if p == 0 else device(x, y, z + 4 + step, c)

    def x_copy(self, ch, p, rel):
        x, y, z, c = self.at
        here = self.rows(p, self.at[1 + p])
        return remote(
            self.own.at[ch, here],
            self.full.at[ch, rel - 1, here],
            self.xs.at[ch, p, rel - 1],
            self.xr.at[ch, p, rel - 1],
            device(x + 4 - rel, y, z, c),
        )

    def a_copy(self, ch, p, d, arriving=False):
        step = 1 - 2 * d
        pos = self.at[1 + p] - step if arriving else self.at[1 + p]
        ref = self.full.at[ch, :, self.rows(p, pos)]
        return remote(ref, ref, self.as_.at[ch, p, d], self.ar.at[ch, p, d], self.near(p, step))

    def b_copy(self, ch, p, d, arriving=False):
        step = 1 - 2 * d
        pos = self.at[1 + p] - 2 if arriving else self.at[1 + p] - step
        ref = self.full.at[ch, :, self.rows(p, pos), pl.ds(d * (D // 2), D // 2)]
        return remote(ref, ref, self.bs.at[ch, p, d], self.br.at[ch, p, d], self.near(p, step))

    def c_copy(self, ch, arriving=False):
        x, y, z, c = self.at
        half = 1 - c if arriving else c
        ref = self.full.at[ch, :, pl.ds(pl.multiple_of(half * HALF, 8), HALF)]
        return remote(ref, ref, self.cs.at[ch], self.cr.at[ch], device(x, y, z, 1 - c))

    def send(self, ch):
        for p in (0, 1):
            for rel in (1, 3, 2):
                self.x_copy(ch, p, rel).start()

    def from_x(self, k):
        for p in (0, 1):
            for rel in (1, 2, 3):
                self.x_copy(k, p, rel).wait_recv()
        for p, d in self.BOTH:
            self.a_copy(k, p, d).start()

    def onward(self, k):
        for p, d in self.BOTH:
            self.a_copy(k, p, d, True).wait_recv()
        for p, d in self.BOTH:
            self.b_copy(k, p, d).start()

    def to_core(self, k):
        for p, d in self.BOTH:
            self.b_copy(k, p, d, True).wait_recv()
        self.c_copy(k).start()

    def go(self, *steps):
        for step in steps:
            (self.from_x, self.onward, self.to_core)["xoc".index(step[0])](int(step[1:]))

    def arrive(self, ch):
        self.c_copy(ch, True).wait_recv()

    def end(self):
        def sent(ch):
            for p in (0, 1):
                for rel in (1, 2, 3):
                    self.x_copy(ch, p, rel).wait_send()
            for p, d in self.BOTH:
                self.a_copy(ch, p, d).wait_send()
                self.b_copy(ch, p, d).wait_send()
            self.c_copy(ch).wait_send()

        loop(CHUNKS, sent)


class Nowhere:
    end = lambda self: None
    send = arrive = lambda self, k: None
    go = lambda self, *steps: None


PAIR_AT = (0, 256, 384, 512)
THIRD_AT = (128, 192, 640, 704)


def repack_heads(st, wb):
    for a in range(2):
        for r in range(4):
            to, third = a * 768 + PAIR_AT[r], a * 768 + THIRD_AT[r]
            wb[to : to + 128] = st[r, a * 192 : a * 192 + 128].astype(bf)
            wb[third : third + 64] = st[r, a * 192 + 128 : a * 192 + 192].astype(bf)


def repack_hidden(st, wb):
    for a in range(3):
        for r in range(4):
            to = a * 512 + r * 128
            wb[to : to + 128] = st[r, a * 128 : a * 128 + 128].astype(bf)


def transpose_to(dst, src):
    for t in range(NB):
        dst[:, t * T : (t + 1) * T] = src[t * T : (t + 1) * T, :].T


def rms(r):
    return lax.rsqrt(jnp.mean(r * r, axis=-1, keepdims=True) + EPS)


def rope(v, cs, sl, sr):
    return v * cs + pltpu.roll(v, 96, 1) * sl + pltpu.roll(v, 32, 1) * sr


def rope_sides(sn):
    first = (lane(sn.shape) % 64) < 32
    return jnp.where(first, -sn, 0.0), jnp.where(first, 0.0, sn)


def head_lanes(h, shape):
    at = lane(shape)
    mine = at < 64 if h == 0 else at >= 64
    base = 64 if h == 0 else 0
    return mine, at - base


def project_scores(u, w, cs, sn, length, qa, ka, k):
    def step(t):
        at = block(t, 512)
        ut = u[at]
        c = cs[at]
        sl, sr = rope_sides(sn[at])
        shape = (512, 128)
        bias = jnp.where(line(shape) + t * 512 < length, 0.0, NEG)
        val = nt(ut, w[0:768])
        for p in range(6):
            q_p = rope(val[:, p * 128 : p * 128 + 128], c, sl, sr)
            for h in range(2):
                mine, side = head_lanes(h, shape)
                qa[2 * p + h, at] = jnp.where(mine, q_p, jnp.where(side == 0, 1.0, 0.0)).astype(bf)
        val = nt(ut, w[768:1536])
        for p in range(6):
            k_p = rope(val[:, p * 128 : p * 128 + 128], c, sl, sr)
            k[p, at] = k_p.astype(bf)
            for h in range(2):
                mine, side = head_lanes(h, shape)
                other = jnp.where(side == 0, bias, jnp.where(side < 4, -1.0, 0.0))
                ka[2 * p + h, at] = jnp.where(mine, k_p, other).astype(bf)

    loop(2, step)


def project_values(u, w, va, v):
    def step(t):
        at = block(t, 512)
        val = nt(u[at], w[0:768])
        for p in range(6):
            v_p = val[:, p * 128 : p * 128 + 128]
            v[p, at] = v_p.astype(bf)
            for h in range(2):
                mine, side = head_lanes(h, (512, 128))
                va[2 * p + h, at] = jnp.where(mine, v_p, jnp.where((side >= 1) & (side < 4), -1.0, 0.0)).astype(bf)

    loop(2, step)


def attend(qa, ka, vt, o, ob, lse, tick):
    def pair(p):
        at_l = pl.ds(pl.multiple_of(p * 128, 128), 128)
        for i in range(NB):
            n = (i + 1) * T
            rows = pl.ds(i * T, T)
            diag = line((T, T)) <= lane((T, T))
            outs, outl = [], []
            for h in range(2):
                s = nt(ka[2 * p + h, 0:n], qa[2 * p + h, rows])
                tail = jnp.where(diag, s[n - T :], NEG)
                s = tail if i == 0 else jnp.concatenate([s[: n - T], tail], axis=0)
                m = jnp.max(s, axis=0, keepdims=True) * SCALE2
                e = jnp.exp2(s * SCALE2 - m)
                tot = jnp.sum(e, axis=0, keepdims=True)
                pr = e * (1.0 / tot)
                pb = pr.astype(bf)
                main = nn(vt[p, h * 64 : h * 64 + 64, 0:n], pb)
                rest = (pr - pb.astype(f32)).astype(bf)
                outs.append(main)
                outl.append(main + nn(vt[p, h * 64 : h * 64 + 64, 0:n], rest))
                lse[pl.ds(p * 2 + h, 1), rows] = m + jnp.log2(tot)
            ob[rows, at_l] = jnp.concatenate(outs, axis=0).T.astype(bf)
            o[rows, at_l] = jnp.concatenate(outl, axis=0).T
        tick(p)

    loop(6, pair)


def three(v):
    hi = v.astype(bf).astype(f32)
    mid = (v - hi).astype(bf).astype(f32)
    low = (v - hi - mid).astype(bf).astype(f32)
    return (hi + pltpu.roll(mid, 16, 1) + pltpu.roll(low, 32, 1)).astype(bf)


def spread_table():
    table = np.zeros((128, 12 * 128), np.float32)
    for h in range(12):
        for j in range(3):
            table[16 * j + h, h * 128 + (65 if h % 2 == 0 else 1) + j] = 1.0
    return table.astype(ml_dtypes.bfloat16)


FWD_OUT = [
    ((CHUNKS, 1536, D), bf),
    ((2, 2, D, S), bf),
    ((2, 12, S, 128), bf),
    ((2, 12, S, 128), bf),
    ((2, 12, S, 128), bf),
    ((2, 6, 128, S), bf),
    ((2, S, D), f32),
    ((2, S, 256), bf),
    ((2, 4, S, 512), bf),
    ((2, 4, S, 512), bf),
    ((2, 4, S, 128), bf),
    ((4, S, D), f32),
    ((S, D), f32),
]
FWD_VMEM = [
    ((S, D), f32),
    ((2, 4, ROWS, D), f32),
    ((2, 1536, D), bf),
    ((12, S, 128), bf),
    ((12, S, 128), bf),
    ((12, S, 128), bf),
    ((6, S, 128), bf),
    ((6, S, 128), bf),
    ((6, 128, S), bf),
    ((6, 128, S), bf),
    ((S, D), f32),
    ((S, D), bf),
    ((128, S), f32),
    ((S, D), bf),
    ((2, D, S), bf),
    ((S, D), f32),
    ((S, D), f32),
    ((2, 2, 512, 512), bf),
    ((4, S, 128), bf),
    ((3, 192, D), bf),
    ((192, D), bf),
    ((2, D, 512), bf),
    ((512, D), bf),
]


def fwd_kernel(comm, length_ref, wq, wk, wv, wo, wg, wu, wd, x_hbm, cs, sn, gains, spread, *rest):
    own, full, rest = (rest[1], rest[0], rest[2:]) if not comm else (rest[0], rest[1], rest[2:])
    outs, rest = rest[: len(FWD_OUT)], rest[len(FWD_OUT) :]
    w_o, ut_o, qa_o, ka_o, va_o, kt_o, o_o, ob_o, a_o, b_o, hb_o, res_o, out_o = outs
    (x, st, wb, qa, ka, va, k, v, kt, vt, o, ob, lse, u, ut, acc, res, ab, hb, raw_h, raw_o, raw_f, raw_d), rest = (
        rest[: len(FWD_VMEM)],
        rest[len(FWD_VMEM) :],
    )
    load_sem, w_sem, save_sem, ab_sem, own_sem, put_sem = rest[:6]
    net = Gather(own, full, rest[6:]) if comm else Nowhere()
    length = length_ref[0]

    def raw(layer, i):
        src = (wq, wk, wv, wo, wg, wu, wd)[i]
        dst = (raw_h.at[0], raw_h.at[1], raw_h.at[2], raw_o, raw_f.at[0], raw_f.at[1], raw_d)[i]
        return pltpu.make_async_copy(src.at[layer], dst, own_sem.at[i])

    def own_chunks(layer):
        if layer == 0:
            return [st.at[i // 4, i % 4] for i in range(6)]
        return [st.at[1, 2], st.at[1, 3]] + [b.at[pl.ds(i * ROWS, ROWS)] for b in (acc, res) for i in range(2)]

    def put_own(layer, i):
        return pltpu.make_async_copy(own_chunks(layer)[i], own.at[layer * 6 + i], put_sem.at[i])

    def turn(dst, row, src):
        for t in range(3):
            dst[row : row + src.shape[1], t * T : (t + 1) * T] = src[t * T : (t + 1) * T, :].astype(f32).T

    def start_raw(layer):
        for i in range(7):
            raw(layer, i).start()

    def prepare_heads(layer):
        to = own_chunks(layer)
        for n in range(2):
            raw(layer, 2 * n).wait()
            raw(layer, 2 * n + 1).wait()
            to[n][0:192] = raw_h[2 * n].astype(f32)
            to[n][192:384] = (raw_o if n else raw_h.at[1])[...].astype(f32)
            put_own(layer, n).start()

    def prepare_hidden(layer):
        to = own_chunks(layer)
        for i in (4, 5, 6):
            raw(layer, i).wait()
        for f in range(4):
            for i in range(2):
                turn(to[2 + f], i * 128, raw_f.at[i, :, pl.ds(f * 128, 128)])
            to[2 + f][256:384] = raw_d[f * 128 : f * 128 + 128].astype(f32)
            put_own(layer, 2 + f).start()

    def send_own(layer, chunks):
        for i in chunks:
            put_own(layer, i).wait()
            net.send(layer * 6 + i)

    if comm:
        greet()
    start_raw(0)
    x_in = pltpu.make_async_copy(x_hbm, x, save_sem.at[0])
    x_in.start()
    prepare_heads(0)
    if comm:
        greeted()
    send_own(0, (0, 1))
    prepare_hidden(0)
    start_raw(1)
    send_own(0, (2, 3, 4, 5))
    prepare_heads(1)
    prepare_hidden(1)
    send_own(1, range(6))
    x_in.wait()

    def loads(ch, slot):
        return (
            pltpu.make_async_copy(own.at[ch], st.at[slot, 0], load_sem.at[slot, 0]),
            pltpu.make_async_copy(full.at[ch], st.at[slot, pl.ds(1, 3)], load_sem.at[slot, 1]),
        )

    def start_load(ch, slot):
        net.arrive(ch)
        for copy in loads(ch, slot):
            copy.start()

    def put_weights(ch, slot):
        return pltpu.make_async_copy(wb.at[slot], w_o.at[ch], w_sem.at[slot])

    def unpack(ch, slot, repack, first=False):
        for copy in loads(ch, slot):
            copy.wait()
        if not first:
            put_weights(ch, slot).wait()
        repack(st.at[slot], wb.at[slot])
        put_weights(ch, slot).start()

    flying = {}

    def save(name, src, dst, i):
        flying[name] = pltpu.make_async_copy(src, dst, save_sem.at[i])
        flying[name].start()

    def settle(*names):
        for name in names:
            if name in flying:
                flying.pop(name).wait()

    lse[...] = jnp.zeros((128, S), f32)
    for layer in range(2):
        base = layer * 6
        settle("uta")

        def enter(t):
            at = block(t)
            val = x[at]
            if layer:
                val = val * rms(val) * gains[2:3]
            u[at] = val.astype(bf)

        loop(NB, enter)
        transpose_to(ut.at[0], u)
        save("uta", ut.at[0], ut_o.at[layer, 0], 0)
        if layer == 0:
            net.go("x0", "x1", "o0", "o1", "x2", "c0", "c1")
            start_load(0, 0)
        unpack(base, 0, repack_heads, layer == 0)
        settle("qa", "ka", "va", "kt", "o", "ob")
        project_scores(u, wb.at[0], cs, sn, length, qa, ka, k)
        if layer == 0:
            start_load(1, 1)
        unpack(base + 1, 1, repack_heads, layer == 0)
        project_values(u, wb.at[1], va, v)
        for p in range(6):
            transpose_to(kt.at[p], k.at[p])
            transpose_to(vt.at[p], v.at[p])
        save("ka", ka, ka_o.at[layer], 1)
        save("va", va, va_o.at[layer], 2)
        save("kt", kt, kt_o.at[layer], 3)
        net.go(*(("x10", "o8") if layer else ("x3", "o2")))

        def tick(p):
            plans = (
                {1: ("x4", "o3"), 3: ("x5", "c2", "o4"), 5: ("x6", "c3", "o5")},
                {1: ("x11", "o9"), 3: ("o10", "c8"), 5: ("o11", "c9")},
            )
            for at, plan in plans[layer].items():

                @pl.when(p == at)
                def _():
                    net.go(*plan)

        attend(qa, ka, vt, o, ob, lse, tick)
        start_load(base + 2, 0)
        save("o", o, o_o.at[layer], 4)
        save("ob", ob.at[:, pl.ds(0, 256)], ob_o.at[layer], 5)

        def add_lse(t):
            at = block(t, 512)
            val = nn(three(lse[:, at].T * (1.0 / SCALE2)), spread[...]).astype(bf)
            for h in range(12):
                qa[h, at] = qa[h, at] + val[:, h * 128 : h * 128 + 128]

        loop(2, add_lse)
        save("qa", qa, qa_o.at[layer], 6)
        settle("res")

        def after(t):
            at = block(t, 512)
            r = x[at] + nn(ob[at], wb[1, 768:1536])
            res[at] = r
            n = r * rms(r)
            if layer == 0:
                h = n * gains[0:1]
                acc[at] = h
                u[at] = h.astype(bf)
            else:
                acc[at] = r
                u[at] = (n * gains[3:4]).astype(bf)

        loop(2, after)
        save("res", res, res_o.at[2 * layer if layer == 0 else 3], 7)
        settle("utf")
        transpose_to(ut.at[1], u)
        save("utf", ut.at[1], ut_o.at[layer, 1], 8)
        settle("hb")
        net.go(*(("c10", "c11") if layer else ("x7", "c4", "o6")))

        def chunk(f):
            ch = base + 2 + f
            slot = lax.rem(f, 2)

            if layer == 0:
                for at, plan in {1: ("o7", "c5"), 2: ("x8", "c6"), 3: ("c7",)}.items():

                    @pl.when(f == at)
                    def _():
                        net.go(*plan)

            @pl.when(ch + 1 < CHUNKS)
            def _():
                start_load(ch + 1, 1 - slot)

            unpack(ch, slot, repack_hidden)
            w = wb.at[slot]

            def put(t, j):
                return pltpu.make_async_copy(
                    ab.at[t, j], (a_o, b_o)[j].at[layer, f, pl.ds(t * 512, 512)], ab_sem.at[t, j]
                )

            @pl.when(f >= 1)
            def _():
                for t in range(2):
                    put(t, 0).wait()
                    put(t, 1).wait()

            for t in range(2):
                at = pl.ds(t * 512, 512)
                ub = u[at]
                gate = nt(ub, w[0:512])
                up = nt(ub, w[512:1024])
                sig = 1.0 / (1.0 + jnp.exp(-gate))
                a = gate * sig
                hid = (a * up).astype(bf)
                ab[t, 0] = a.astype(bf)
                ab[t, 1] = (up * (sig + a * (1.0 - sig))).astype(bf)
                hb[f, at] = hid[:, 0:128]
                acc[at] = acc[at] + nn(hid, w[1024:1536])
            for t in range(2):
                put(t, 0).start()
                put(t, 1).start()

        loop(4, chunk)
        for t in range(2):
            for j in range(2):
                pltpu.make_async_copy(ab.at[t, j], a_o.at[layer, 0, block(0, 512)], ab_sem.at[t, j]).wait()
        save("hb", hb, hb_o.at[layer], 9)
        if layer == 0:
            net.go("x9")
            start_load(7, 1)
            settle("res")

            def leave(t):
                at = block(t)
                r = acc[at]
                res[at] = r
                x[at] = r * rms(r) * gains[1:2]

            loop(NB, leave)
            save("res", res, res_o.at[1], 7)
            save("y", x, res_o.at[2], 10)
        else:
            settle("y")

            def last(t):
                at = block(t)
                x[at] = jnp.where(line((T, 1)) + t * T < length, acc[at], 0.0)

            loop(NB, last)
            save("out", x, out_o, 11)
    settle(*list(flying))
    for slot in range(2):
        put_weights(0, slot).wait()
    net.end()


def whole(memory):
    return pl.BlockSpec(memory_space=memory)


def forward(length, weights, x, cs, sn, gains, spread, full=None):
    comm = full is None
    hbm, vmem = whole(pl.ANY), whole(pltpu.VMEM)
    extra = [((CHUNKS, ROWS, D), f32)] + ([((CHUNKS, 3, ROWS, D), f32)] if comm else [])
    outs = [jax.ShapeDtypeStruct(s, d) for s, d in extra + FWD_OUT]
    dma = pltpu.SemaphoreType.DMA
    result = pl.pallas_call(
        lambda *refs: fwd_kernel(comm, *refs),
        out_shape=outs,
        in_specs=[whole(pltpu.SMEM)] + [hbm] * 8 + [vmem] * 4 + ([] if comm else [hbm]),
        out_specs=[hbm] * len(outs),
        scratch_shapes=[pltpu.VMEM(s, d) for s, d in FWD_VMEM]
        + [dma((2, 2)), dma((2,)), dma((12,)), dma((2, 2)), dma((7,)), dma((6,))]
        + ([dma(s) for s in Gather.SEMS] if comm else []),
        compiler_params=pltpu.CompilerParams(
            vmem_limit_bytes=63 * 2**20,
            **(dict(collective_id=0, has_side_effects=True) if comm else {}),
        ),
    )(length, *weights, x, cs, sn, gains, spread, *([] if comm else [full]))
    return result[len(extra) :]


GROUPS = 6
GRAD_ROWS = 24


class Scatter:
    SEMS = [(GROUPS,)] * 2 + [(GROUPS, 2, 3)] * 4 + [(7,)] * 2
    VMEM = [
        ((2, 2, 16, GRAD_ROWS, D), f32),
        ((4, 16, GRAD_ROWS, D), f32),
        ((2, 2, 3, 4, GRAD_ROWS, D // 2), f32),
        ((2, 2, 3, GRAD_ROWS, D // 2), f32),
        ((8, D), f32),
        ((7, 8, D), f32),
    ]

    def __init__(self, out, bufs, sems):
        self.out = out
        self.grads, self.sums, self.one, self.two, self.gain, self.gains_in = bufs
        self.cs, self.cr, self.s1, self.r1, self.s2, self.r2, self.gs, self.gr = sems
        self.at = place()

    def peer(self, along, k):
        x, y, z, c = self.at
        return device(x, y + k, z, c) if along == 0 else device(x, y, z + k, c)

    def greet(self):
        x, y, z, c = self.at
        bar = pltpu.get_barrier_semaphore()
        to = [self.peer(a, k) for a in (0, 1) for k in (1, 2, 3)] + [device(x, y, z, 1 - c)]
        for other in to:
            pl.semaphore_signal(bar, inc=1, device_id=other, device_id_type=MESH)

    def greeted(self):
        pl.semaphore_wait(pltpu.get_barrier_semaphore(), 7)

    def columns(self, part):
        return pl.ds(part * (D // 2), D // 2)

    def core_copy(self, g):
        x, y, z, c = self.at
        return remote(
            self.grads.at[lax.rem(g, 2), 1 - c],
            self.sums.at[lax.rem(g, 4)],
            self.cs.at[g],
            self.cr.at[g],
            device(x, y, z, 1 - c),
        )

    def four(self, g, part, pos):
        ref = self.sums.at[lax.rem(g, 4)]
        if part == 0:
            return ref.at[pl.ds(pos * 4, 4), :, self.columns(0)]
        return ref

    def one_copies(self, g, part, k):
        pos = lax.rem(self.at[1 + part] + k, 4)
        slot = lax.rem(g, 2)
        dst = self.one.at[slot, part, 3 - k]
        send, recv, to = self.s1.at[g, part, k - 1], self.r1.at[g, part, 3 - k], self.peer(part, k)
        sums = self.sums.at[lax.rem(g, 4)]
        if part == 0:
            return [remote(sums.at[pl.ds(pos * 4, 4), :, self.columns(0)], dst, send, recv, to)]
        return [remote(sums.at[i * 4 + pos, :, self.columns(1)], dst.at[i], send, recv, to) for i in range(4)]

    def one_wait(self, g, part, k):
        dst = self.one.at[lax.rem(g, 2), part, k - 1]
        return remote(dst, dst, self.s1.at[g, part, k - 1], self.r1.at[g, part, k - 1], self.peer(part, k))

    def two_copy(self, g, part, k):
        along = 1 - part
        pos = lax.rem(self.at[1 + along] + k, 4)
        _, y, z, _ = self.at
        index = y * 4 + pos if part == 0 else pos * 4 + z
        return remote(
            self.sums.at[lax.rem(g, 4), index, :, self.columns(part)],
            self.two.at[lax.rem(g, 2), part, 3 - k],
            self.s2.at[g, part, k - 1],
            self.r2.at[g, part, 3 - k],
            self.peer(along, k),
        )

    def two_wait(self, g, part, k):
        dst = self.two.at[lax.rem(g, 2), part, k - 1]
        return remote(dst, dst, self.s2.at[g, part, k - 1], self.r2.at[g, part, k - 1], self.peer(1 - part, k))

    def gain_copy(self, step, k=0):
        x, y, z, c = self.at
        if step == 0:
            i = j = 0
            to = device(x, y, z, 1 - c)
        else:
            i, j = 3 * step - 3 + k, 3 * step - 3 + 4 - k
            to = self.peer(step - 1, k)
        return remote(self.gain, self.gains_in.at[j], self.gs.at[i], self.gr.at[j], to)

    def stage0(self, g):
        self.core_copy(g).start()

    def stage1(self, g):
        copy = self.core_copy(g)
        copy.wait_recv()
        c = self.at[3]
        slot, ring = lax.rem(g, 2), lax.rem(g, 4)

        def add(i):
            self.sums[ring, i] = self.sums[ring, i] + self.grads[slot, c, i]

        loop(16, add)
        for part in (0, 1):
            for k in (1, 3, 2):
                for one in self.one_copies(g, part, k):
                    one.start()
        copy.wait_send()

    def stage2(self, g):
        for part in (0, 1):
            for k in (1, 2, 3):
                self.one_wait(g, part, k).wait_recv()
        _, y, z, _ = self.at
        slot, ring = lax.rem(g, 2), lax.rem(g, 4)

        def add(i):
            for part in (0, 1):
                at = (y * 4 + i) if part == 0 else (i * 4 + z)
                cols = pl.ds(part * (D // 2), D // 2)
                got = self.one[slot, part, 0, i] + self.one[slot, part, 1, i] + self.one[slot, part, 2, i]
                self.sums[ring, at, :, cols] = self.sums[ring, at, :, cols] + got

        for part in (0, 1):
            for k in (1, 2, 3):
                self.one_sent(g, part, k)
        loop(4, add)
        for part in (0, 1):
            for k in (1, 3, 2):
                self.two_copy(g, part, k).start()

    def one_sent(self, g, part, k):
        for one in self.one_copies(g, part, k):
            one.wait_send()

    def stage3(self, g):
        for part in (0, 1):
            for k in (1, 2, 3):
                self.two_wait(g, part, k).wait_recv()
        _, y, z, _ = self.at
        slot, ring = lax.rem(g, 2), lax.rem(g, 4)
        for part in (0, 1):
            cols = pl.ds(part * (D // 2), D // 2)
            got = self.two[slot, part, 0] + self.two[slot, part, 1] + self.two[slot, part, 2]
            self.out[g, :, cols] = self.sums[ring, y * 4 + z, :, cols] + got
        for part in (0, 1):
            for k in (1, 2, 3):
                self.two_copy(g, part, k).wait_send()

    def tick(self, n):
        @pl.when((n >= 3) & (n < GROUPS + 3))
        def _():
            self.stage3(n - 3)

        @pl.when((n >= 2) & (n < GROUPS + 2))
        def _():
            self.stage2(n - 2)

        @pl.when((n >= 1) & (n < GROUPS + 1))
        def _():
            self.stage1(n - 1)

        @pl.when(n < GROUPS)
        def _():
            self.stage0(n)

    def gain_start(self, step):
        if step == 0:
            self.gain_copy(0).start()
        else:
            for k in (1, 2, 3):
                self.gain_copy(step, k).start()

    def gain_finish(self, step):
        copies = [self.gain_copy(0)] if step == 0 else [self.gain_copy(step, k) for k in (1, 2, 3)]
        for copy in copies:
            copy.wait()
        first = 0 if step == 0 else 3 * step - 2
        for j in range(first, first + len(copies)):
            self.gain[...] = self.gain[...] + self.gains_in[j]


class Keep:
    VMEM = Scatter.VMEM

    def __init__(self, out, bufs, sems):
        self.out, self.grads, self.gain, self.sem = out, bufs[0], bufs[4], sems[0]

    def greet(self):
        pass

    greeted = greet

    def tick(self, n):
        @pl.when(n < GROUPS)
        def _():
            copy = pltpu.make_async_copy(self.grads.at[lax.rem(n, 2)], self.out.at[n], self.sem)
            copy.start()
            copy.wait()

    def gain_start(self, step):
        pass

    gain_finish = gain_start


BWD_VMEM = [
    ((S, D), f32),
    ((S, D), f32),
    ((S, D), f32),
    ((S, D), f32),
    ((S, D), bf),
    ((D, S), bf),
    ((D, S), bf),
    ((2, 1536, D), bf),
    ((2, 2, 512, 512), bf),
    ((12, S, 128), bf),
    ((12, S, 128), bf),
    ((12, S, 128), bf),
    ((12, S, 128), bf),
    ((6, 128, S), bf),
    ((S, D), bf),
    ((S, D), bf),
    ((S, D), bf),
    ((128, S), f32),
    ((4, S, 256), bf),
]


def bwd_kernel(comm, length_ref, cot, w, uts, qas, kas, vas, kts, os_, obs, as_, bs, hbs, ress, cs, sn, gains, spread, *rest):
    input_grad, gain_out, grad_out = rest[:3]
    rest = rest[3:]
    (e, acc, res, mix, eb, ebt, ut, wb, ab, qa, ka, va, da, kt, dq, dk, dv, dqt, own), rest = (
        rest[: len(BWD_VMEM)],
        rest[len(BWD_VMEM) :],
    )
    bufs, rest = rest[: len(Scatter.VMEM)], rest[len(Scatter.VMEM) :]
    load_sem, w_sem, ab_sem, rest = rest[0], rest[1], rest[2], rest[3:]
    net = (Scatter if comm else Keep)(grad_out, bufs, rest)
    grads, gain = bufs[0], bufs[4]
    length = length_ref[0]

    flying = {}

    def fetch(name, src, dst, i):
        flying[name] = pltpu.make_async_copy(src, dst, load_sem.at[i])
        flying[name].start()

    def need(*names):
        for name in names:
            flying.pop(name).wait()

    def weights(ch, slot):
        return pltpu.make_async_copy(w.at[ch], wb.at[slot], w_sem.at[slot])

    def factors(layer, f, t):
        return [
            pltpu.make_async_copy(src.at[layer, f, block(t, 512)], ab.at[t, j], ab_sem.at[t, j])
            for j, src in ((0, as_), (1, bs))
        ]

    def round_grad():
        def step(t):
            at = block(t)
            eb[at] = e[at].astype(bf)

        loop(NB, step)
        transpose_to(ebt, eb)

    def norm_back(incoming, r, row):
        fac = rms(r)
        n = r * fac
        gain[row : row + 1] = gain[row : row + 1] + jnp.sum(incoming * n, axis=0, keepdims=True)
        inner = incoming * gains[row : row + 1]
        return fac * (inner - n * jnp.mean(inner * n, axis=-1, keepdims=True))

    def place_rows(slot, i, cols, val):
        for b in range(16):
            grads[slot, b % 2, i * 8 + b // 2, :, cols] = val[b * 24 : b * 24 + 24]

    def heads_in(layer):
        fetch("qa", qas.at[layer], qa, 3)
        fetch("ka", kas.at[layer], ka, 4)
        fetch("va", vas.at[layer], va, 5)
        fetch("kt", kts.at[layer], kt, 6)
        fetch("mix", os_.at[layer], mix, 9)

    net.greet()
    gain[...] = jnp.zeros((8, D), f32)
    fetch("cot", cot, e, 0)
    fetch("ut", uts.at[1, 1], ut, 1)
    fetch("res", ress.at[3], res, 2)
    weights(8, 0).start()
    for t in range(2):
        for copy in factors(1, 0, t):
            copy.start()
    need("cot")

    def mask(t):
        at = block(t)
        e[at] = jnp.where(line((T, 1)) + t * T < length, e[at], 0.0)

    loop(NB, mask)
    heads_in(1)

    for layer in (1, 0):
        base = layer * 6
        group = 3 * (1 - layer)
        round_grad()

        def clear(t):
            acc[block(t)] = jnp.zeros((T, D), f32)

        loop(NB, clear)
        need("ut")
        if layer:
            net.greeted()

        def half(hh):
            for i in range(2):
                pltpu.make_async_copy(
                    hbs.at[layer, 2 * hh + i], own.at[2, :, pl.ds(i * 128, 128)], load_sem.at[10 + i]
                ).start()

            for i in range(2):
                f = 2 * hh + i
                ch = base + 2 + f
                weights(ch, i).wait()
                if i == 0:
                    weights(ch + 1, 1).start()
                else:

                    @pl.when(hh == 0)
                    def _():
                        weights(ch + 1, 0).start()

                    @pl.when(hh == 1)
                    def _():
                        weights(base, 0).start()

                def step(t):
                    at = block(t, 512)
                    for copy in factors(layer, f, t):
                        copy.wait()
                    a, b = ab[t, 0].astype(f32), ab[t, 1].astype(f32)
                    dh = nt(eb[at], wb[i, 1024:1536])
                    dg = (dh * b).astype(bf)
                    du = (dh * a).astype(bf)
                    own[0, at, i * 128 : i * 128 + 128] = dg[:, 0:128]
                    own[1, at, i * 128 : i * 128 + 128] = du[:, 0:128]
                    acc[at] = acc[at] + nn(dg, wb[i, 0:512]) + nn(du, wb[i, 512:1024])

                    @pl.when(f < 3)
                    def _():
                        for copy in factors(layer, f + 1, t):
                            copy.start()

                loop(2, step)
            for i in range(2):
                pltpu.make_async_copy(
                    hbs.at[layer, 2 * hh + i], own.at[2, :, pl.ds(i * 128, 128)], load_sem.at[10 + i]
                ).wait()
            slot = lax.rem(group + hh, 2)

            def outer(i):
                at = block(i, 384)
                vals = nn(ut[at], own[0]), nn(ut[at], own[1]), nn(ebt[at], own[2])
                for n in range(3):
                    place_rows(slot, i, pl.ds(n * 256, 256), vals[n])

            loop(2, outer)
            net.tick(group + hh)

        loop(2, half)
        weights(base + 1, 1).start()
        fetch("ut", uts.at[layer, 0], ut, 1)
        fetch("ob", obs.at[layer], own.at[3], 7)
        need("res")

        def through(t):
            at = block(t)
            if layer:
                e[at] = e[at] + norm_back(acc[at], res[at], 3)
            else:
                e[at] = norm_back(e[at] + acc[at], res[at], 0)

        loop(NB, through)
        if layer:
            fetch("res", ress.at[2], res, 2)
        round_grad()
        if layer == 0:
            net.gain_start(0)
        weights(base, 0).wait()
        weights(base + 1, 1).wait()
        need("mix")
        owner = jnp.where(line((D, 128)) // 64 == lane((D, 128)), 1.0, 0.0).astype(bf)

        def mixed_back(t):
            at = block(t, 512)
            val = nt(eb[at], wb[1, 768:1536]).astype(bf)
            prod = val.astype(f32) * mix[at]
            hi = prod.astype(bf)
            low = (prod - hi.astype(f32)).astype(bf)
            inner = nn(three(nn(hi, owner) + nn(low, owner)), spread[...])
            for h in range(12):
                mine, _ = head_lanes(h % 2, (512, 128))
                pair = val[:, (h // 2) * 128 : (h // 2) * 128 + 128]
                da[h, at] = jnp.where(mine, pair, inner[:, h * 128 : h * 128 + 128].astype(bf))

        loop(2, mixed_back)
        if layer:
            fetch("below", ress.at[1], mix, 9)
        need("qa", "ka", "va", "kt", "ut", "ob")
        low = lane((T, 128)) < 64

        def pair(p):
            at_l = pl.ds(pl.multiple_of(p * 128, 128), 128)
            for j in range(NB):
                ks, qs = pl.ds(j * T, T), pl.ds(j * T, S - j * T)
                diag = line((T, T)) <= lane((T, T))
                dvs, dks = [], []
                for h in range(2):
                    hd = 2 * p + h
                    s = nt(ka[hd, ks], qa[hd, qs])
                    dp = nt(va[hd, ks], da[hd, qs])
                    pr = jnp.exp2(s * SCALE2)
                    head = jnp.where(diag, pr[:, :T], 0.0)
                    pr = head if j == NB - 1 else jnp.concatenate([head, pr[:, T:]], axis=1)
                    ds = (pr * dp).astype(bf)
                    dvs.append(nn(pr.astype(bf), da[hd, qs]))
                    dks.append(nn(ds, qa[hd, qs]))
                    val = nn(kt[p, h * 64 : h * 64 + 64, ks], ds)
                    if j == 0:
                        dqt[h * 64 : h * 64 + 64, :] = val
                    else:
                        dqt[h * 64 : h * 64 + 64, j * T :] = dqt[h * 64 : h * 64 + 64, j * T :] + val
                dv[ks, at_l] = jnp.where(low, dvs[0], dvs[1]).astype(bf)
                sl, sr = rope_sides(sn[ks])
                dk_j = jnp.where(low, dks[0], dks[1]) * 0.125
                dk[ks, at_l] = rope(dk_j, cs[ks], -sl, -sr).astype(bf)
            for j in range(NB):
                ks = pl.ds(j * T, T)
                sl, sr = rope_sides(sn[ks])
                dq_j = dqt[:, j * T : j * T + T].T * 0.125
                dq[ks, at_l] = rope(dq_j, cs[ks], -sl, -sr).astype(bf)

        loop(2, pair)
        slot = (group + 2) % 2

        def own_heads(i):
            at = block(i, 384)
            vals = [nn(ut[at], dq[:, 0:256]), nn(ut[at], dk[:, 0:256]), nn(ut[at], dv[:, 0:256]), nn(ebt[at], own[3])]
            left = lane((384, 128)) < 64
            tiles = [v[:, 0:128] for v in vals] + [
                jnp.where(left, vals[n][:, 128:256], pltpu.roll(vals[n + 1][:, 128:256], 64, 1)) for n in (0, 2)
            ]
            for n, tile in enumerate(tiles):
                place_rows(slot, i, pl.ds(n * 128, 128), tile)

        loop(2, own_heads)
        net.tick(group + 2)
        if layer:
            fetch("ut", uts.at[0, 1], ut, 1)
            loop(4, lambda p: pair(p + 2))
        else:
            net.gain_finish(0)
            net.gain_start(1)
            loop(2, lambda p: pair(p + 2))
            net.tick(6)
            net.gain_finish(1)
            net.gain_start(2)
            loop(2, lambda p: pair(p + 4))
            net.tick(7)
            net.gain_finish(2)

        def into(t):
            at = block(t, 512)
            val = nn(dq[at], wb[0, 0:768]) + nn(dk[at], wb[0, 768:1536]) + nn(dv[at], wb[1, 0:768])
            acc[at] = val

        loop(2, into)
        if layer:
            weights(2, 0).start()
            for t in range(2):
                for copy in factors(0, 0, t):
                    copy.start()
            need("res", "below")

            def between(t):
                at = block(t)
                e[at] = norm_back(e[at] + norm_back(acc[at], res[at], 2), mix[at], 1)

            loop(NB, between)
            fetch("res", ress.at[0], res, 2)
            heads_in(0)
        else:

            def last(t):
                at = block(t)
                acc[at] = e[at] + acc[at]

            loop(NB, last)
            done = pltpu.make_async_copy(acc, input_grad, load_sem.at[0])
            done.start()
            gain_out[...] = gain[...]
            net.tick(8)
            done.wait()


def backward(comm, length, cot, kept, cs, sn, gains, spread):
    hbm, vmem = whole(pl.ANY), whole(pltpu.VMEM)
    dma = pltpu.SemaphoreType.DMA
    w, uts, qas, kas, vas, kts, os_, obs, as_, bs, hbs, ress = kept[:12]
    grad = (GROUPS, GRAD_ROWS, D) if comm else (GROUPS, 2, 16, GRAD_ROWS, D)
    return pl.pallas_call(
        lambda *refs: bwd_kernel(comm, *refs),
        out_shape=[jax.ShapeDtypeStruct(s, f32) for s in [(S, D), (8, D), grad]],
        in_specs=[whole(pltpu.SMEM)] + [hbm] * 13 + [vmem] * 4,
        out_specs=[hbm, vmem, vmem if comm else hbm],
        scratch_shapes=[pltpu.VMEM(s, d) for s, d in BWD_VMEM + Scatter.VMEM]
        + [dma((12,)), dma((2,)), dma((2, 2))]
        + ([dma(s) for s in Scatter.SEMS] if comm else [dma]),
        compiler_params=pltpu.CompilerParams(
            vmem_limit_bytes=63 * 2**20,
            **(dict(collective_id=1, has_side_effects=True) if comm else {}),
        ),
    )(length, cot, w, uts, qas, kas, vas, kts, os_, obs, as_, bs, hbs, ress, cs, sn, gains, spread)


def finish_kernel(out_in, grad_in, sums, gain, out, grad, q, k, v, o, gate, up, down, gains, last, big, sem):
    parts = [(src, dst, t) for src, dst in ((out_in, out), (grad_in, grad)) for t in range(NB)]

    def get(n):
        src, _, t = parts[n]
        return pltpu.make_async_copy(src.at[pl.ds(t * T, T)], big.at[n], sem.at[n])

    def put(n):
        _, dst, t = parts[n]
        return pltpu.make_async_copy(big.at[n], dst.at[pl.ds(t * T, T)], sem.at[n])

    for n in range(len(parts)):
        get(n).start()
    for layer in range(2):
        heads = sums.at[5 - 3 * layer]
        thirds = [heads[:, 512:640], heads[:, 640:768]]
        thirds = [thirds[0], pltpu.roll(thirds[0], 64, 1), thirds[1], pltpu.roll(thirds[1], 64, 1)]
        for n, to in enumerate((q, k, v, o)):
            to[layer, :, 0:128] = heads[:, n * 128 : n * 128 + 128]
            to[layer, :, 128:192] = thirds[n][:, 0:64]
        for half in range(2):
            for n, to in enumerate((gate, up, down)):
                to[layer, :, half * 256 : half * 256 + 256] = sums[3 - 3 * layer + half, :, n * 256 : n * 256 + 256]
    mine = pltpu.roll(gain[...], lax.rem(D - lax.axis_index("dp") * GRAD_ROWS, D), 1)
    gains[...] = mine[0:3, 0:GRAD_ROWS]
    last[...] = mine[3:4, 0:GRAD_ROWS]
    for n in range(len(parts)):
        get(n).wait()
        put(n).start()
    for n in range(len(parts)):
        put(n).wait()


def finish(out, grad, sums, gain):
    hbm, vmem = whole(pl.ANY), whole(pltpu.VMEM)
    shapes = [(S, D)] * 2 + [(2, GRAD_ROWS, 192)] * 4 + [(2, GRAD_ROWS, 512)] * 3 + [(3, GRAD_ROWS), (1, GRAD_ROWS)]
    return pl.pallas_call(
        finish_kernel,
        out_shape=[jax.ShapeDtypeStruct(s, f32) for s in shapes],
        in_specs=[hbm, hbm, vmem, vmem],
        out_specs=[hbm, hbm] + [vmem] * 9,
        scratch_shapes=[pltpu.VMEM((2 * NB, T, D), f32), pltpu.SemaphoreType.DMA((2 * NB,))],
        compiler_params=pltpu.CompilerParams(vmem_limit_bytes=60 * 2**20),
    )(out, grad, sums, gain)


def rope_tables():
    freq = (10000.0 ** (-np.arange(32) * 2.0 / 64)).astype(np.float32)
    angle = (np.arange(S, dtype=np.float32)[:, None] * freq[None, :]).astype(np.float64)
    return tuple(np.tile(v.astype(np.float32), (1, 4)) for v in (np.cos(angle), np.sin(angle)))


def local(block_input, lengths, cotangent, w_query, w_key, w_value, w_output, w_gate, w_up, w_down, gains):
    cs, sn = rope_tables()
    spread = spread_table()
    heads = [jnp.swapaxes(w, 1, 2) for w in (w_query, w_key, w_value)]
    weights = (*heads, w_output, w_gate, w_up, w_down)
    kept = forward(lengths, weights, block_input, cs, sn, gains, spread)
    input_grad, gain_sums, grads = backward(True, lengths, cotangent, kept, cs, sn, gains, spread)
    out, input_grad, q, k, v, o, gate, up, down, gain_grads, last = finish(kept[12], input_grad, grads, gain_sums)
    return (out, input_grad, q, k, v, jnp.swapaxes(o, 1, 2), gate, up, jnp.swapaxes(down, 1, 2), gain_grads, last[0])


def solution(mesh):
    rows, cols, deep = P("dp", None), P(None, None, "tensor"), P(None, "tensor", None)
    return jax.shard_map(
        local,
        mesh=mesh,
        in_specs=(rows, P("dp"), rows, cols, cols, cols, deep, cols, cols, deep, P()),
        out_specs=(rows, rows)
        + (P(None, "dp", "tensor"),) * 3
        + (P(None, "tensor", "dp"),)
        + (P(None, "dp", "tensor"),) * 2
        + (P(None, "tensor", "dp"), P(None, "dp"), P("dp")),
        check_vma=False,
    )
```
